32 devices in a mesh: prop: 16 (over z, y, x), trans: 2 (over core).
Axes of the slice: x: 2, y: 2, z: 4, core: 2. Of those that a mesh axis runs over, the one named last changes fastest.
Arguments:
- velocity: float32 [3, 128, 32, 128], P(None, 'prop', 'trans'), may hold values from -4 to 4
- stress: float32 [6, 128, 32, 128], P(None, 'prop', 'trans'), may hold values from -4 to 4
- density: float32 [12, 128, 32, 128], P(None, 'prop', 'trans'), may hold values from 0.5 to 2
- shear: float32 [128, 32, 128], P('prop', 'trans'), may hold values from 0.5 to 2
- normals: int32 [12, 3], replicated, may hold values from -2 to 2, as said below
- directions: int32 [12, 3], replicated, may hold values from -2 to 2, as said below
- inflow: float32 [21, 4, 32, 128], P(None, None, 'trans'), may hold values from -1.4 to 1.4
Outputs:
- velocity_out: float32 [3, 128, 32, 128], P(None, 'prop', 'trans')
- stress_out: float32 [6, 128, 32, 128], P(None, 'prop', 'trans')
- density_out: float32 [12, 128, 32, 128], P(None, 'prop', 'trans')
The draws below stay inside these ranges and needn't reach their ends.
Inputs may be any that keep to these rules, and one draw needn't show every extreme that they name: `normals`: every entry of each normal is nonzero. `directions`: each direction has exactly one zero entry and is perpendicular to the normal of the same row.
All inputs are finite; a program needn't handle non-finite values.
Results may differ from the reference program's by a relative error of at most 0.00015.
Values sent between devices are 32-bit elements; how exact they have to be, the bound alone decides.
No kernel may reach another device: no remote copies, remote signals or barrier semaphores. Data moves between devices by JAX's collectives and lax.ppermute only.
A program may use at most 64 MiB of HBM per device.

```python
import math
import jax
import jax.numpy as jnp
from jax import lax

NZ = 128
SLIPS = 12
STEPS = 4
ADV = 4
FIELDS = 21
NX = 128
NY = 32


def slip_draws(key):
    magnitude = jax.random.randint(jax.random.fold_in(key, 11), (SLIPS, 3), 1, 3)
    signs = 2 * jax.random.randint(jax.random.fold_in(key, 13), (SLIPS, 3), 0, 2) - 1
    normal_rows = (magnitude * signs).astype(jnp.int32)
    which_form = jax.random.randint(jax.random.fold_in(key, 17), (SLIPS,), 0, 3)
    orient = 2 * jax.random.randint(jax.random.fold_in(key, 19), (SLIPS,), 0, 2) - 1
    first = normal_rows[:, 0]
    second = normal_rows[:, 1]
    third = normal_rows[:, 2]
    nothing = 0 * first
    form_zero = jnp.stack([second, -first, nothing], 1)
    form_one = jnp.stack([third, nothing, -first], 1)
    form_two = jnp.stack([nothing, third, -second], 1)
    chosen = jnp.where((which_form == 0)[:, None], form_zero, jnp.where((which_form == 1)[:, None], form_one, form_two))
    return (normal_rows, (chosen * orient[:, None]).astype(jnp.int32))


def draw_normals(key, part):
    return slip_draws(key)[0]


def draw_directions(key, part):
    return slip_draws(key)[1]


def levels(stream_key, dims, shards, least, top_value):
    def one(dim, parts):
        steps = jax.random.uniform(jax.random.fold_in(jax.random.fold_in(stream_key, 6), dim), (parts,), jnp.float32, least / len(shards), top_value / len(shards))
        return jnp.repeat(jnp.exp(steps), dims[dim] // parts).reshape((-1,) + (1,) * (len(dims) - dim - 1))

    level = one(*shards[0])
    for cut in shards[1:]:
        level = level * one(*cut)
    return level


def gaussian(key, extent, deviation, reach, shards=(), dtype=jnp.bfloat16):
    loudness = levels(key, extent, shards, -0.22, 0.18) if shards else 1.0
    values = jax.random.normal(key, extent, jnp.float32) * deviation * loudness
    return jnp.minimum(jnp.maximum(values, -reach), reach).astype(dtype)


def setup_inputs(seed: int = 0) -> dict:
    splits = jax.random.split(jax.random.key(seed), 8)
    velocity = gaussian(splits[0], (3, NX, NY, NZ), 1.0, 4.0, ((1, 16), (2, 2)), jnp.float32)
    stress = gaussian(splits[1], (6, NX, NY, NZ), 1.0, 4.0, ((1, 16), (2, 2)), jnp.float32)
    density = jnp.clip(jnp.exp(math.log(2.0) - 1.3862944 * jax.random.uniform(splits[2], (SLIPS, NX, NY, NZ), jnp.float32) ** levels(splits[2], (SLIPS, NX, NY, NZ), ((1, 16), (2, 2)), -0.2, 0.2)), 0.5, 2.0)
    shear = jnp.clip(jnp.exp(math.log(2.0) - 1.3862944 * jax.random.uniform(splits[3], (NX, NY, NZ), jnp.float32) ** levels(splits[3], (NX, NY, NZ), ((0, 16), (1, 2)), -0.2, 0.2)), 0.5, 2.0)
    normals = draw_normals(jax.random.fold_in(splits[7], 71), 0)
    directions = draw_directions(jax.random.fold_in(splits[7], 71), 0)
    inflow = gaussian(splits[6], (FIELDS, ADV, NY, NZ), 0.5, 1.4, ((2, 2),), jnp.float32)
    return dict(velocity=velocity, stress=stress, density=density, shear=shear, normals=normals, directions=directions, inflow=inflow)


TIME_STEP = 0.15
DRAG_RATE = 0.5
HARDENING = 2.0
RECOVERY = 1.0
VOIGT_PAIRS = ((0, 0), (1, 1), (2, 2), (1, 2), (0, 2), (0, 1))

def derivative(field, which_axis):
    if which_axis == 3:
        field = jnp.pad(field, ((0, 0), (0, 0), (0, 0), (2, 2)))
    length = field.shape[which_axis] - 4

    def offset_slice(offset):
        return lax.slice_in_dim(field, 2 + offset, 2 + offset + length, axis=which_axis)
    result = (8.0 * (offset_slice(1) - offset_slice(-1)) - (offset_slice(2) - offset_slice(-2))) / 12.0
    for other_axis in (1, 2):
        if other_axis != which_axis:
            result = lax.slice_in_dim(result, 2, result.shape[other_axis] - 2, axis=other_axis)
    return result

def schmid_table(normals, directions):
    normal_f = normals.astype(jnp.float32)
    direct_f = directions.astype(jnp.float32)
    scale = 1.0 / (jnp.sqrt(lax.optimization_barrier(jnp.sum(normal_f * normal_f, 1))) * jnp.sqrt(lax.optimization_barrier(jnp.sum(direct_f * direct_f, 1))))
    columns = [0.5 * (direct_f[:, i] * normal_f[:, j] + direct_f[:, j] * normal_f[:, i]) * scale for i, j in VOIGT_PAIRS]
    return jnp.stack(columns, 1)

def accelerate(velocity_inner, stress_padded):
    part_x = derivative(jnp.stack([stress_padded[0], stress_padded[5], stress_padded[4]]), 1)
    part_y = derivative(jnp.stack([stress_padded[5], stress_padded[1], stress_padded[3]]), 2)
    part_z = derivative(jnp.stack([stress_padded[4], stress_padded[3], stress_padded[2]]), 3)
    return velocity_inner + TIME_STEP * (part_x + part_y + part_z)

def plastic_update(stress, density, shear, velocity_padded, table):
    grad_x = derivative(velocity_padded, 1)
    grad_y = derivative(velocity_padded, 2)
    grad_z = derivative(velocity_padded, 3)
    strain = jnp.stack([grad_x[0], grad_y[1], grad_z[2], 0.5 * (grad_y[2] + grad_z[1]), 0.5 * (grad_x[2] + grad_z[0]), 0.5 * (grad_x[1] + grad_y[0])])
    weights = jnp.array([1.0, 1.0, 1.0, 2.0, 2.0, 2.0], jnp.float32)
    resolved = jnp.einsum('sk,kxyz->sxyz', table * weights, stress, precision=lax.Precision.HIGHEST)
    slip_rate = DRAG_RATE * density * jnp.tanh(resolved)
    plastic = jnp.einsum('sk,sxyz->kxyz', table, slip_rate, precision=lax.Precision.HIGHEST)
    elastic = strain - plastic
    dilation = shear * (elastic[0] + elastic[1] + elastic[2])
    increment = 2.0 * shear * elastic
    increment = jnp.concatenate([increment[:3] + dilation, increment[3:]], 0)
    stress_new = stress + TIME_STEP * increment
    growth = TIME_STEP * jnp.abs(slip_rate) * (HARDENING * lax.rsqrt(density) - RECOVERY)
    return (stress_new, density * jnp.exp(growth))

def pad_sides(field):
    return jnp.pad(field, ((0, 0), (2, 2), (2, 2), (0, 0)))

def reference(velocity, stress, density, shear, normals, directions, inflow):
    table = schmid_table(normals, directions)
    for turn_index in range(STEPS):
        velocity_new = accelerate(velocity, pad_sides(stress))
        stress, density = plastic_update(stress, density, shear, pad_sides(velocity_new), table)
        velocity = velocity_new
    velocity_out = jnp.concatenate([velocity[:, ADV:], inflow[:3]], 1)
    stress_out = jnp.concatenate([stress[:, ADV:], inflow[3:9]], 1)
    density_out = jnp.concatenate([density[:, ADV:], inflow[9:]], 1)
    return (velocity_out, stress_out, density_out)
```

```python
import functools

import jax
import jax.numpy as jnp
from jax import lax
from jax.experimental import pallas as pl
from jax.experimental.pallas import tpu as pltpu
from jax.sharding import PartitionSpec as P

STEPS = 4
ADV = 4
TIME_STEP = 0.15
DRAG_RATE = 0.5
HARDENING = 2.0
RECOVERY = 1.0
VOIGT_PAIRS = ((0, 0), (1, 1), (2, 2), (1, 2), (0, 2), (0, 1))
ACCEL = ((0, 5, 4), (5, 1, 3), (4, 3, 2))

PLANES = 8
ROWS = 16
TAIL = 8
EXT = ROWS + TAIL
LANES = 128
C1 = TIME_STEP / 12.0
C8 = 8.0 * TIME_STEP / 12.0
F32 = jnp.float32


def lane_shifts(x):
    lane = lax.broadcasted_iota(jnp.int32, x.shape, 1)

    def at(offset):
        moved = pltpu.roll(x, (-offset) % LANES, 1)
        inside = lane < LANES - offset if offset > 0 else lane >= -offset
        return jnp.where(inside, moved, 0.0)

    return at(1) - at(-1), at(2) - at(-2)


def row_shifts(x):
    size = x.shape[0]
    return (
        pltpu.roll(x, size - 1, 0) - pltpu.roll(x, 1, 0),
        pltpu.roll(x, size - 2, 0) - pltpu.roll(x, 2, 0),
    )


def extended(inner, tail):
    return jnp.concatenate([inner, tail], axis=0)


def edge_tile(plane):
    row = lax.broadcasted_iota(jnp.int32, (TAIL, LANES), 0)
    return jnp.where(row < 4, plane[:TAIL], plane[ROWS - TAIL :])


def plastic_parts(stress, densities, shear, tab_ref):
    doubled = [s if k < 3 else s + s for k, s in enumerate(stress)]
    total = [None] * 6
    grown = []
    for s in range(12):
        coef = [tab_ref[s, k] for k in range(6)]
        coef = [jnp.concatenate([c] * (stress[0].shape[0] // 8), axis=0) for c in coef]
        resolved = doubled[0] * coef[0]
        for k in range(1, 6):
            resolved = resolved + doubled[k] * coef[k]
        density = densities(s)
        rate = (DRAG_RATE * density) * jnp.tanh(resolved)
        for k in range(6):
            term = rate * coef[k]
            total[k] = term if total[k] is None else total[k] + term
        growth = (TIME_STEP * jnp.abs(rate)) * (HARDENING * lax.rsqrt(density) - RECOVERY)
        grown.append(density * jnp.exp(growth))
    scaled = TIME_STEP * shear
    dilation = scaled * (total[0] + total[1] + total[2])
    twice = 2.0 * scaled
    left = [stress[k] - twice * total[k] - (dilation if k < 3 else 0.0) for k in range(6)]
    return left, grown


def stress_change(near, velocity, shear):
    grad = [[None] * 3 for _ in range(3)]
    for c in range(3):
        first = near(c, 1) - near(c, -1)
        second = near(c, 2) - near(c, -2)
        grad[0][c] = 8.0 * first - second
        first, second = row_shifts(velocity[c])
        grad[1][c] = 8.0 * first[:ROWS] - second[:ROWS]
        first, second = lane_shifts(velocity[c][:ROWS])
        grad[2][c] = 8.0 * first - second
    scaled = C1 * shear
    trace = grad[0][0] + grad[1][1] + grad[2][2]
    return [
        scaled * (trace + 2.0 * grad[0][0]),
        scaled * (trace + 2.0 * grad[1][1]),
        scaled * (trace + 2.0 * grad[2][2]),
        scaled * (grad[1][2] + grad[2][1]),
        scaled * (grad[0][2] + grad[2][0]),
        scaled * (grad[0][1] + grad[1][0]),
    ]


def edges_kernel(v_ref, s_ref, edge_ref):
    for p in range(PLANES):
        for c in range(3):
            edge_ref[c, p] = edge_tile(v_ref[c, p])
        for k in range(6):
            edge_ref[3 + k, p] = edge_tile(s_ref[k, p])


def partial_update(p, v_ref, s_ref, rec_ref, below):
    out = []
    for c, (ix, iy, iz) in enumerate(ACCEL):

        def plane(k, q):
            return extended(s_ref[k, q], rec_ref[3 + k, q])

        along = extended(s_ref[iy, p], rec_ref[3 + iy, p] * below)
        first, second = row_shifts(along)
        f, s = lane_shifts(plane(iz, p))
        first, second = first + f, second + s
        if p + 1 < PLANES:
            first = first + plane(ix, p + 1)
        if p - 1 >= 0:
            first = first - plane(ix, p - 1)
        if p + 2 < PLANES:
            second = second + plane(ix, p + 2)
        if p - 2 >= 0:
            second = second - plane(ix, p - 2)
        start = extended(v_ref[c, p], rec_ref[c, p])
        out.append(start + C8 * first - C1 * second)
    return out


def first_kernel(v_ref, s_ref, rec_ref, mask_ref, w_ref, near_ref, far_ref):
    below = mask_ref[0]
    even = mask_ref[3] > 0.5
    for p in range(PLANES):
        made = partial_update(p, v_ref, s_ref, rec_ref, below)
        for c in range(3):
            w_ref[c, p] = made[c]
    for q in range(2):
        low, high = q, PLANES - 2 + q
        for c in range(3):
            for h in range(2):
                rows = pl.ds(8 * h, 8)
                left, right = w_ref[c, low, rows], w_ref[c, high, rows]
                near_ref[q, 2 * c + h] = jnp.where(even, right, left)
                far_ref[q, 2 * c + h] = jnp.where(even, left, right)
                left, right = s_ref[ACCEL[c][0], low, rows], s_ref[ACCEL[c][0], high, rows]
                near_ref[q, 6 + 3 * c + h] = jnp.where(even, right, left)
                far_ref[q, 6 + 3 * c + h] = jnp.where(even, left, right)
            left, right = rec_ref[3 + ACCEL[c][0], low], rec_ref[3 + ACCEL[c][0], high]
            near_ref[q, 6 + 3 * c + 2] = jnp.where(even, right, left)
            far_ref[q, 6 + 3 * c + 2] = jnp.where(even, left, right)


def plastic_kernel(ahead, s_ref, d_ref, shear_ref, tab_ref, left_ref, grown_ref, *send_ref):
    for p in range(PLANES):
        left, grown = plastic_parts(
            [s_ref[k, p] for k in range(6)], lambda s: d_ref[s, p], shear_ref[p], tab_ref
        )
        for k in range(6):
            left_ref[k, p] = left[k]
        for s in range(12):
            grown_ref[s, p] = grown[s]
            if ahead and p < ADV:
                send_ref[0][s, p] = grown[s]
        if ahead and p < ADV:
            send_ref[0][12, p] = shear_ref[p]


def second_kernel(
    w_ref, near_ref, far_ref, s_ref, left_ref, shear_ref, mask_ref, v_ref, out_ref, edge_ref, vel
):
    below, has_left, has_right = mask_ref[0], mask_ref[1], mask_ref[2]
    even = mask_ref[3] > 0.5

    def got(side, q, tile):
        a, b = near_ref[q, tile], far_ref[q, tile]
        return jnp.where(even, b, a) if side == 0 else jnp.where(even, a, b)

    def got_w(side, q, c):
        return jnp.concatenate([got(side, q, 2 * c + h) for h in range(2)], axis=0)

    def got_s(side, q, c):
        return jnp.concatenate([got(side, q, 6 + 3 * c + h) for h in range(3)], axis=0)

    exists = [jnp.concatenate([m, m], axis=0) for m in (has_left, has_right)]
    for c in range(3):
        ix = ACCEL[c][0]
        m2, m1, p8, p9 = got_s(0, 0, c), got_s(0, 1, c), got_s(1, 0, c), got_s(1, 1, c)
        for p in range(PLANES):
            value = w_ref[c, p]
            if p == 0:
                value = value - C8 * m1 + C1 * m2
            if p == 1:
                value = value + C1 * m1
            if p == 6:
                value = value - C1 * p8
            if p == 7:
                value = value + C8 * p8 - C1 * p9
            value = extended(value[:ROWS], value[ROWS:] * below)
            vel[c, p + 2] = value
            v_ref[c, p] = value[:ROWS]
            edge_ref[c, p] = edge_tile(value[:ROWS])
        none = jnp.zeros((TAIL, LANES), F32)
        halo = (
            (0, got_w(0, 0, c) - C1 * s_ref[ix, 0], 0),
            (1, got_w(0, 1, c) + C8 * s_ref[ix, 0] - C1 * s_ref[ix, 1], 0),
            (10, got_w(1, 0, c) - C8 * s_ref[ix, 7] + C1 * s_ref[ix, 6], 1),
            (11, got_w(1, 1, c) + C1 * s_ref[ix, 7], 1),
        )
        for at, value, side in halo:
            vel[c, at] = extended(value * exists[side], none)
    for p in range(PLANES):
        change = stress_change(
            lambda c, o: vel[c, p + 2 + o, pl.ds(0, ROWS)], [vel[c, p + 2] for c in range(3)], shear_ref[p]
        )
        for k in range(6):
            value = left_ref[k, p] + change[k]
            out_ref[k, p] = value
            edge_ref[3 + k, p] = edge_tile(value)


LAST_W, LAST_S, LAST_X, LAST_TILES = 0, 48, 96, 102


def last_first_kernel(v_ref, s_ref, rec_ref, mask_ref, w_ref, msg_ref):
    below = mask_ref[0]
    for p in range(PLANES):
        made = partial_update(p, v_ref, s_ref, rec_ref, below)
        for c in range(3):
            w_ref[c, p] = made[c]
            if p < 6:
                base = LAST_W + 16 * c + (3 * p if p < 4 else 12 + 2 * (p - 4))
                for h in range(3 if p < 4 else 2):
                    msg_ref[base + h] = made[c][8 * h : 8 * h + 8]
            if p < 2:
                msg_ref[LAST_X + 2 * c + p] = rec_ref[3 + ACCEL[c][0], p]
        if p < ADV:
            for k in range(6):
                for h in range(2):
                    msg_ref[LAST_S + 8 * k + 2 * p + h] = s_ref[k, p, pl.ds(8 * h, 8)]


def last_plastic_kernel(s_ref, d_ref, shear_ref, tab_ref, left_ref, grown_ref):
    for p in range(ADV, PLANES):
        left, grown = plastic_parts(
            [s_ref[k, p] for k in range(6)], lambda s: d_ref[s, p], shear_ref[p], tab_ref
        )
        for k in range(6):
            left_ref[k, p - ADV] = left[k]
        for s in range(12):
            grown_ref[s, p - ADV] = grown[s]


def last_second_kernel(
    w_ref, msg_ref, more_ref, s_ref, rec_ref, left_ref, grown_ref, shear_ref, tab_ref, mask_ref, inflow_ref,
    v_ref, out_ref, d_ref, vel,
):
    below = mask_ref[0]
    here = jnp.concatenate([mask_ref[2]] * 2, axis=0)
    inside = here > 0.5

    def got(base, count):
        return jnp.concatenate([msg_ref[base + h] for h in range(count)], axis=0)

    def got_stress(k, p):
        return got(LAST_S + 8 * k + 2 * p, 2)

    for c in range(3):
        ix = ACCEL[c][0]
        p8 = extended(got_stress(ix, 0), msg_ref[LAST_X + 2 * c])
        p9 = extended(got_stress(ix, 1), msg_ref[LAST_X + 2 * c + 1])
        p6 = extended(s_ref[ix, 6], rec_ref[3 + ix, 6])
        p7 = extended(s_ref[ix, 7], rec_ref[3 + ix, 7])
        for p in range(2, 14):
            if p < PLANES:
                value = w_ref[c, p]
                if p == 6:
                    value = value - C1 * p8
                if p == 7:
                    value = value + C8 * p8 - C1 * p9
            elif p < 12:
                value = got(LAST_W + 16 * c + 3 * (p - 8), 3)
                if p == 8:
                    value = value - C8 * p7 + C1 * p6
                if p == 9:
                    value = value + C1 * p7
            else:
                value = got(LAST_W + 16 * c + 12 + 2 * (p - 12), 2)
            inner = value[:ROWS]
            tail = value[ROWS:] * below if p < 12 else jnp.zeros((TAIL, LANES), F32)
            if p >= PLANES:
                inner, tail = inner * here, tail * mask_ref[2]
            vel[c, p - 2] = extended(inner, tail)
            if ADV <= p < 12:
                if p >= PLANES:
                    inner = jnp.where(inside, inner, inflow_ref[c, p - PLANES])
                v_ref[c, p - ADV] = inner
    for q in range(PLANES):
        p = q + ADV
        if p < PLANES:
            left = [left_ref[k, q] for k in range(6)]
            grown = [grown_ref[s, q] for s in range(12)]
            shear = shear_ref[p]
        else:
            r = p - PLANES
            shear = more_ref[12, r]
            left, grown = plastic_parts(
                [got_stress(k, r) for k in range(6)], lambda s: more_ref[s, r], shear, tab_ref
            )
        change = stress_change(
            lambda c, o: vel[c, p - 2 + o, pl.ds(0, ROWS)], [vel[c, p - 2] for c in range(3)], shear
        )
        for k in range(6):
            value = left[k] + change[k]
            if p >= PLANES:
                value = jnp.where(inside, value, inflow_ref[3 + k, p - PLANES])
            out_ref[k, q] = value
        for s in range(12):
            value = grown[s]
            if p >= PLANES:
                value = jnp.where(inside, value, inflow_ref[9 + s, p - PLANES])
            d_ref[s, q] = value


VMEM_LIMIT = 16 * 2**20


def call(kernel, outs, args, scratch=(), flops=0):
    return pl.pallas_call(
        kernel,
        out_shape=[jax.ShapeDtypeStruct(shape, F32) for shape in outs],
        scratch_shapes=[pltpu.VMEM(shape, F32) for shape in scratch],
        compiler_params=pltpu.CompilerParams(vmem_limit_bytes=VMEM_LIMIT),
        cost_estimate=pl.CostEstimate(flops=flops, bytes_accessed=2**20, transcendentals=0),
    )(*args)


def schmid_table(normals, directions):
    normal_f = normals.astype(F32)
    direct_f = directions.astype(F32)
    scale = 1.0 / (
        jnp.sqrt(jnp.sum(normal_f * normal_f, 1)) * jnp.sqrt(jnp.sum(direct_f * direct_f, 1))
    )
    columns = [
        0.5 * (direct_f[:, i] * normal_f[:, j] + direct_f[:, j] * normal_f[:, i]) * scale
        for i, j in VOIGT_PAIRS
    ]
    return jnp.stack(columns, 1)


def swap_rows(edge):
    count = lax.axis_size("trans")
    if count == 2:
        return lax.ppermute(edge, "trans", [(0, 1), (1, 0)])
    upper = lax.ppermute(edge[:, :, :4], "trans", [(i + 1, i) for i in range(count - 1)])
    lower = lax.ppermute(edge[:, :, 4:], "trans", [(i, i + 1) for i in range(count - 1)])
    return jnp.concatenate([upper, lower], axis=2)


def local(velocity, stress, density, shear, normals, directions, inflow):
    count = lax.axis_size("prop")
    at, side = lax.axis_index("prop"), lax.axis_index("trans")
    table = jnp.broadcast_to(schmid_table(normals, directions)[:, :, None, None], (12, 6, 8, LANES))
    row = lax.broadcasted_iota(jnp.int32, (TAIL, LANES), 0)
    full = jnp.ones((TAIL, LANES), F32)
    masks = jnp.stack(
        [
            jnp.where(row < 4, side < lax.axis_size("trans") - 1, side > 0).astype(F32),
            full * (at > 0).astype(F32),
            full * (at < count - 1).astype(F32),
            full * (at % 2 == 0).astype(F32),
        ]
    )
    pairs = [(i, i + 1) for i in range(0, count - 1, 2)]
    others = [(i, i + 1) for i in range(1, count - 1, 2)]
    pairs, others = ([(a, b) for a, b in p] + [(b, a) for a, b in p] for p in (pairs, others))

    shape = (PLANES, ROWS, LANES)
    wide = (3, PLANES, EXT, LANES)
    edge_shape = (9, PLANES, TAIL, LANES)
    (edge,) = call(edges_kernel, [edge_shape], (velocity, stress))
    for step in range(STEPS - 1):
        rec = swap_rows(edge)
        message = (2, 15, 8, LANES)
        w, near, far = call(first_kernel, [wide, message, message], (velocity, stress, rec, masks))
        far = lax.ppermute(far, "prop", others)
        near = lax.ppermute(near, "prop", pairs)
        ahead = step == STEPS - 2
        made = call(
            functools.partial(plastic_kernel, ahead),
            [(6, *shape), (12, *shape)] + ([(13, ADV, ROWS, LANES)] if ahead else []),
            (stress, density, shear, table),
            flops=2**24,
        )
        left, density = made[:2]
        if ahead:
            more = lax.ppermute(made[2], "prop", [(i + 1, i) for i in range(count - 1)])
        velocity, stress, edge = call(
            second_kernel,
            [(3, *shape), (6, *shape), edge_shape],
            (w, near, far, stress, left, shear, masks),
            scratch=[(3, PLANES + 4, EXT, LANES)],
        )
    rec = swap_rows(edge)
    w, message = call(
        last_first_kernel, [wide, (LAST_TILES, 8, LANES)], (velocity, stress, rec, masks)
    )
    message = lax.ppermute(message, "prop", [(i + 1, i) for i in range(count - 1)])
    half = (ADV, ROWS, LANES)
    left, grown = call(
        last_plastic_kernel, [(6, *half), (12, *half)], (stress, density, shear, table), flops=2**23
    )
    return tuple(
        call(
            last_second_kernel,
            [(3, *shape), (6, *shape), (12, *shape)],
            (w, message, more, stress, rec, left, grown, shear, table, masks, inflow),
            scratch=[(3, PLANES + 4, EXT, LANES)],
        )
    )


def solution(mesh):
    return jax.shard_map(
        local,
        mesh=mesh,
        in_specs=(
            P(None, "prop", "trans", None),
            P(None, "prop", "trans", None),
            P(None, "prop", "trans", None),
            P("prop", "trans", None),
            P(),
            P(),
            P(None, None, "trans", None),
        ),
        out_specs=(
            P(None, "prop", "trans", None),
            P(None, "prop", "trans", None),
            P(None, "prop", "trans", None),
        ),
        check_vma=False,
    )
```

```python
import functools

import jax
import jax.numpy as jnp
from jax import lax
from jax.experimental import pallas as pl
from jax.experimental.pallas import tpu as pltpu
from jax.sharding import PartitionSpec as P

STEPS = 4
ADV = 4
TIME_STEP = 0.15
DRAG_RATE = 0.5
HARDENING = 2.0
RECOVERY = 1.0
VOIGT_PAIRS = ((0, 0), (1, 1), (2, 2), (1, 2), (0, 2), (0, 1))
ACCEL = ((0, 5, 4), (5, 1, 3), (4, 3, 2))

PLANES = 8
ROWS = 16
TAIL = 8
EXT = ROWS + TAIL
LANES = 128
C1 = TIME_STEP / 12.0
C8 = 8.0 * TIME_STEP / 12.0
F32 = jnp.float32


def lane_shifts(x):
    lane = lax.broadcasted_iota(jnp.int32, x.shape, 1)

    def at(offset):
        moved = pltpu.roll(x, (-offset) % LANES, 1)
        inside = lane < LANES - offset if offset > 0 else lane >= -offset
        return jnp.where(inside, moved, 0.0)

    return at(1) - at(-1), at(2) - at(-2)


def row_shifts(x):
    size = x.shape[0]
    return (
        pltpu.roll(x, size - 1, 0) - pltpu.roll(x, 1, 0),
        pltpu.roll(x, size - 2, 0) - pltpu.roll(x, 2, 0),
    )


def extended(inner, tail):
    return jnp.concatenate([inner, tail], axis=0)


def edge_tile(plane):
    row = lax.broadcasted_iota(jnp.int32, (TAIL, LANES), 0)
    return jnp.where(row < 4, plane[:TAIL], plane[ROWS - TAIL :])


def two_tails(a, b):
    row = lax.broadcasted_iota(jnp.int32, (TAIL, LANES), 0)
    return jnp.where((row < 2) | (row >= 6), a, pltpu.roll(b, 4, 0))


def second_tail(tile):
    return pltpu.roll(tile, 4, 0)


def plastic_parts(stress, densities, shear, tab_ref):
    doubled = [s if k < 3 else s + s for k, s in enumerate(stress)]
    total = [None] * 6
    grown = []
    for s in range(12):
        coef = [tab_ref[s, k] for k in range(6)]
        coef = [jnp.concatenate([c] * (stress[0].shape[0] // 8), axis=0) for c in coef]
        resolved = doubled[0] * coef[0]
        for k in range(1, 6):
            resolved = resolved + doubled[k] * coef[k]
        density = densities(s)
        rate = (DRAG_RATE * density) * jnp.tanh(resolved)
        for k in range(6):
            term = rate * coef[k]
            total[k] = term if total[k] is None else total[k] + term
        growth = (TIME_STEP * jnp.abs(rate)) * (HARDENING * lax.rsqrt(density) - RECOVERY)
        grown.append(density * jnp.exp(growth))
    scaled = TIME_STEP * shear
    dilation = scaled * (total[0] + total[1] + total[2])
    twice = 2.0 * scaled
    left = [stress[k] - twice * total[k] - (dilation if k < 3 else 0.0) for k in range(6)]
    return left, grown


def stress_change(near, velocity, shear):
    grad = [[None] * 3 for _ in range(3)]
    for c in range(3):
        first = near(c, 1) - near(c, -1)
        second = near(c, 2) - near(c, -2)
        grad[0][c] = 8.0 * first - second
        first, second = row_shifts(velocity[c])
        grad[1][c] = 8.0 * first[:ROWS] - second[:ROWS]
        first, second = lane_shifts(velocity[c][:ROWS])
        grad[2][c] = 8.0 * first - second
    scaled = C1 * shear
    trace = grad[0][0] + grad[1][1] + grad[2][2]
    return [
        scaled * (trace + 2.0 * grad[0][0]),
        scaled * (trace + 2.0 * grad[1][1]),
        scaled * (trace + 2.0 * grad[2][2]),
        scaled * (grad[1][2] + grad[2][1]),
        scaled * (grad[0][2] + grad[2][0]),
        scaled * (grad[0][1] + grad[1][0]),
    ]


def edges_kernel(v_in, s_in, edge_ref, v_ref, s_ref, sems):
    copies = [pltpu.make_async_copy(v_in.at[c], v_ref.at[c], sems.at[c]) for c in range(3)]
    copies += [pltpu.make_async_copy(s_in.at[k], s_ref.at[k], sems.at[3 + k]) for k in range(6)]
    for copy in copies:
        copy.start()
    for k, copy in enumerate(copies):
        copy.wait()
        for p in range(PLANES):
            edge_ref[k, p] = edge_tile(v_ref[k, p] if k < 3 else s_ref[k - 3, p])


def partial_update(p, v_ref, s_ref, rec_ref, below):
    out = []
    for c, (ix, iy, iz) in enumerate(ACCEL):

        def plane(k, q):
            return extended(s_ref[k, q], rec_ref[3 + k, q])

        along = extended(s_ref[iy, p], rec_ref[3 + iy, p] * below)
        first, second = row_shifts(along)
        f, s = lane_shifts(plane(iz, p))
        first, second = first + f, second + s
        if p + 1 < PLANES:
            first = first + plane(ix, p + 1)
        if p - 1 >= 0:
            first = first - plane(ix, p - 1)
        if p + 2 < PLANES:
            second = second + plane(ix, p + 2)
        if p - 2 >= 0:
            second = second - plane(ix, p - 2)
        start = extended(v_ref[c, p], rec_ref[c, p])
        out.append(start + C8 * first - C1 * second)
    return out


def first_kernel(v_ref, s_ref, rec_ref, mask_ref, w_ref, near_ref, far_ref):
    below = mask_ref[0]
    even = mask_ref[3] > 0.5
    for p in range(PLANES):
        made = partial_update(p, v_ref, s_ref, rec_ref, below)
        for c in range(3):
            w_ref[c, p] = made[c]
    def both(tile, left, right):
        near_ref[tile] = jnp.where(even, right, left)
        far_ref[tile] = jnp.where(even, left, right)

    low, high = (0, 1), (PLANES - 2, PLANES - 1)
    for c in range(3):
        k = ACCEL[c][0]
        for q in range(2):
            for h in range(2):
                rows = pl.ds(8 * h, 8)
                both(6 * q + 2 * c + h, w_ref[c, low[q], rows], w_ref[c, high[q], rows])
                both(12 + 6 * q + 2 * c + h, s_ref[k, low[q], rows], s_ref[k, high[q], rows])
        left, right = (two_tails(*(rec_ref[3 + k, p] for p in side)) for side in (low, high))
        both(24 + c, left, right)


def plastic_kernel(ahead, s_ref, d_ref, shear_ref, tab_ref, left_ref, grown_ref, *send_ref):
    for p in range(PLANES):
        left, grown = plastic_parts(
            [s_ref[k, p] for k in range(6)], lambda s: d_ref[s, p], shear_ref[p], tab_ref
        )
        for k in range(6):
            left_ref[k, p] = left[k]
        for s in range(12):
            grown_ref[s, p] = grown[s]
            if ahead and p < ADV:
                send_ref[0][s, p] = grown[s]
        if ahead and p < ADV:
            send_ref[0][12, p] = shear_ref[p]


def second_kernel(
    w_ref, far_ref, near_ref, s_ref, left_ref, shear_ref, mask_ref, v_ref, out_ref, edge_ref, vel
):
    below, sides = mask_ref[0], (mask_ref[1], mask_ref[2])
    even = mask_ref[3] > 0.5

    def got(side, tile):
        a, b = near_ref[tile], far_ref[tile]
        return jnp.where(even, b, a) if side == 0 else jnp.where(even, a, b)

    def got_w(side, q, c):
        return jnp.concatenate([got(side, 6 * q + 2 * c + h) for h in range(2)], axis=0)

    def got_s(side, q, c):
        tiles = [got(side, 12 + 6 * q + 2 * c + h) for h in range(2)]
        tail = got(side, 24 + c)
        tiles.append(second_tail(tail) if q else tail)
        return jnp.concatenate([tile * sides[side] for tile in tiles], axis=0)

    exists = [jnp.concatenate([m, m], axis=0) for m in sides]
    for c in range(3):
        ix = ACCEL[c][0]
        m2, m1, p8, p9 = got_s(0, 0, c), got_s(0, 1, c), got_s(1, 0, c), got_s(1, 1, c)
        for p in range(PLANES):
            value = w_ref[c, p]
            if p == 0:
                value = value - C8 * m1 + C1 * m2
            if p == 1:
                value = value + C1 * m1
            if p == 6:
                value = value - C1 * p8
            if p == 7:
                value = value + C8 * p8 - C1 * p9
            value = extended(value[:ROWS], value[ROWS:] * below)
            vel[c, p + 2] = value
            v_ref[c, p] = value[:ROWS]
            edge_ref[c, p] = edge_tile(value[:ROWS])
        none = jnp.zeros((TAIL, LANES), F32)
        halo = (
            (0, got_w(0, 0, c) - C1 * s_ref[ix, 0], 0),
            (1, got_w(0, 1, c) + C8 * s_ref[ix, 0] - C1 * s_ref[ix, 1], 0),
            (10, got_w(1, 0, c) - C8 * s_ref[ix, 7] + C1 * s_ref[ix, 6], 1),
            (11, got_w(1, 1, c) + C1 * s_ref[ix, 7], 1),
        )
        for at, value, side in halo:
            vel[c, at] = extended(value * exists[side], none)
    for p in range(PLANES):
        change = stress_change(
            lambda c, o: vel[c, p + 2 + o, pl.ds(0, ROWS)], [vel[c, p + 2] for c in range(3)], shear_ref[p]
        )
        for k in range(6):
            value = left_ref[k, p] + change[k]
            out_ref[k, p] = value
            edge_ref[3 + k, p] = edge_tile(value)


LAST_W, LAST_S, LAST_T, LAST_X, LAST_TILES = 0, 36, 84, 90, 93


def last_first_kernel(v_ref, s_ref, rec_ref, mask_ref, unused_ref, w_ref, msg_ref):
    below = mask_ref[0]
    for p in range(PLANES):
        made = partial_update(p, v_ref, s_ref, rec_ref, below)
        for c in range(3):
            w_ref[c, p] = made[c]
            if p < 6:
                for h in range(2):
                    msg_ref[LAST_W + 12 * c + 2 * p + h] = made[c][8 * h : 8 * h + 8]
        if p < ADV:
            for k in range(6):
                for h in range(2):
                    msg_ref[LAST_S + 8 * k + 2 * p + h] = s_ref[k, p, pl.ds(8 * h, 8)]
    for c in range(3):
        for q in range(2):
            tails = (w_ref[c, 2 * q + j, pl.ds(ROWS, TAIL)] for j in range(2))
            msg_ref[LAST_T + 2 * c + q] = two_tails(*tails)
        k = 3 + ACCEL[c][0]
        msg_ref[LAST_X + c] = two_tails(rec_ref[k, 0], rec_ref[k, 1])


def last_plastic_kernel(s_ref, d_ref, shear_ref, tab_ref, left_ref, grown_ref):
    for p in range(ADV, PLANES):
        left, grown = plastic_parts(
            [s_ref[k, p] for k in range(6)], lambda s: d_ref[s, p], shear_ref[p], tab_ref
        )
        for k in range(6):
            left_ref[k, p - ADV] = left[k]
        for s in range(12):
            grown_ref[s, p - ADV] = grown[s]


def last_second_kernel(
    w_ref, msg_ref, more_ref, s_ref, rec_ref, left_ref, grown_ref, shear_ref, tab_ref, mask_ref, inflow_ref,
    v_ref, out_ref, d_ref, vel,
):
    below = mask_ref[0]
    here = jnp.concatenate([mask_ref[2]] * 2, axis=0)
    inside = here > 0.5

    def got(base, count):
        return jnp.concatenate([msg_ref[base + h] for h in range(count)], axis=0)

    def got_stress(k, p):
        return got(LAST_S + 8 * k + 2 * p, 2)

    for c in range(3):
        ix = ACCEL[c][0]
        p8 = extended(got_stress(ix, 0), msg_ref[LAST_X + c])
        p9 = extended(got_stress(ix, 1), second_tail(msg_ref[LAST_X + c]))
        p6 = extended(s_ref[ix, 6], rec_ref[3 + ix, 6])
        p7 = extended(s_ref[ix, 7], rec_ref[3 + ix, 7])
        for p in range(2, 14):
            if p < PLANES:
                value = w_ref[c, p]
                if p == 6:
                    value = value - C1 * p8
                if p == 7:
                    value = value + C8 * p8 - C1 * p9
            elif p < 12:
                r = p - PLANES
                tail = msg_ref[LAST_T + 2 * c + r // 2]
                value = extended(got(LAST_W + 12 * c + 2 * r, 2), second_tail(tail) if r % 2 else tail)
                if p == 8:
                    value = value - C8 * p7 + C1 * p6
                if p == 9:
                    value = value + C1 * p7
            else:
                value = got(LAST_W + 12 * c + 2 * (p - PLANES), 2)
            inner = value[:ROWS]
            tail = value[ROWS:] * below if p < 12 else jnp.zeros((TAIL, LANES), F32)
            if p >= PLANES:
                inner, tail = inner * here, tail * mask_ref[2]
            vel[c, p - 2] = extended(inner, tail)
            if ADV <= p < 12:
                if p >= PLANES:
                    inner = jnp.where(inside, inner, inflow_ref[c, p - PLANES])
                v_ref[c, p - ADV] = inner
    for q in range(PLANES):
        p = q + ADV
        if p < PLANES:
            left = [left_ref[k, q] for k in range(6)]
            grown = [grown_ref[s, q] for s in range(12)]
            shear = shear_ref[p]
        else:
            r = p - PLANES
            shear = more_ref[12, r]
            left, grown = plastic_parts(
                [got_stress(k, r) for k in range(6)], lambda s: more_ref[s, r], shear, tab_ref
            )
        change = stress_change(
            lambda c, o: vel[c, p - 2 + o, pl.ds(0, ROWS)], [vel[c, p - 2] for c in range(3)], shear
        )
        for k in range(6):
            value = left[k] + change[k]
            if p >= PLANES:
                value = jnp.where(inside, value, inflow_ref[3 + k, p - PLANES])
            out_ref[k, q] = value
        for s in range(12):
            value = grown[s]
            if p >= PLANES:
                value = jnp.where(inside, value, inflow_ref[9 + s, p - PLANES])
            d_ref[s, q] = value


VMEM_LIMIT = 16 * 2**20
HEAVY = 2**34


def call(kernel, outs, args, scratch=(), flops=0):
    return pl.pallas_call(
        kernel,
        out_shape=[jax.ShapeDtypeStruct(shape, F32) for shape in outs],
        scratch_shapes=[pltpu.VMEM(shape, F32) for shape in scratch],
        compiler_params=pltpu.CompilerParams(vmem_limit_bytes=VMEM_LIMIT),
        cost_estimate=pl.CostEstimate(flops=flops, bytes_accessed=2**20, transcendentals=0),
    )(*args)


def schmid_table(normals, directions):
    normal_f = normals.astype(F32)
    direct_f = directions.astype(F32)
    scale = 1.0 / (
        jnp.sqrt(jnp.sum(normal_f * normal_f, 1)) * jnp.sqrt(jnp.sum(direct_f * direct_f, 1))
    )
    columns = [
        0.5 * (direct_f[:, i] * normal_f[:, j] + direct_f[:, j] * normal_f[:, i]) * scale
        for i, j in VOIGT_PAIRS
    ]
    return jnp.stack(columns, 1)


def swap_rows(edge):
    count = lax.axis_size("trans")
    if count == 2:
        return lax.ppermute(edge, "trans", [(0, 1), (1, 0)])
    upper = lax.ppermute(edge[:, :, :4], "trans", [(i + 1, i) for i in range(count - 1)])
    lower = lax.ppermute(edge[:, :, 4:], "trans", [(i, i + 1) for i in range(count - 1)])
    return jnp.concatenate([upper, lower], axis=2)


def all_trade(pairs, count, width):
    partner = {a: b for a, b in pairs} | {b: a for a, b in pairs}
    out = []
    for i in range(count):
        for t in range(width):
            if i in partner:
                out.append((i * width + t, partner[i] * width + t))
            elif t ^ 1 < width:
                out.append((i * width + t, i * width + (t ^ 1)))
    return out


def local(velocity, stress, density, shear, normals, directions, inflow):
    count = lax.axis_size("prop")
    at, side = lax.axis_index("prop"), lax.axis_index("trans")
    table = jnp.broadcast_to(schmid_table(normals, directions)[:, :, None, None], (12, 6, 8, LANES))
    row = lax.broadcasted_iota(jnp.int32, (TAIL, LANES), 0)
    full = jnp.ones((TAIL, LANES), F32)
    masks = jnp.stack(
        [
            jnp.where(row < 4, side < lax.axis_size("trans") - 1, side > 0).astype(F32),
            full * (at > 0).astype(F32),
            full * (at < count - 1).astype(F32),
            full * (at % 2 == 0).astype(F32),
        ]
    )
    pairs = [(i, i + 1) for i in range(0, count - 1, 2)]
    others = [(i, i + 1) for i in range(1, count - 1, 2)]
    near_swap, far_swap = (all_trade(p, count, lax.axis_size("trans")) for p in (pairs, others))

    shape = (PLANES, ROWS, LANES)
    wide = (3, PLANES, EXT, LANES)
    edge_shape = (9, PLANES, TAIL, LANES)
    edge, velocity, stress = pl.pallas_call(
        edges_kernel,
        out_shape=[jax.ShapeDtypeStruct(d, F32) for d in (edge_shape, (3, *shape), (6, *shape))],
        in_specs=[pl.BlockSpec(memory_space=pltpu.HBM)] * 2,
        scratch_shapes=[pltpu.SemaphoreType.DMA((9,))],
        compiler_params=pltpu.CompilerParams(vmem_limit_bytes=VMEM_LIMIT),
    )(velocity, stress)
    for step in range(STEPS - 1):
        rec = swap_rows(edge)
        message = (27, 8, LANES)
        w, near, far = call(first_kernel, [wide, message, message], (velocity, stress, rec, masks))
        far = lax.ppermute(far, ("prop", "trans"), far_swap)
        near = lax.ppermute(near, ("prop", "trans"), near_swap)
        ahead = step == STEPS - 2
        made = call(
            functools.partial(plastic_kernel, ahead),
            [(6, *shape), (12, *shape)] + ([(13, ADV, ROWS, LANES)] if ahead else []),
            (stress, density, shear, table),
            flops=HEAVY,
        )
        left, density = made[:2]
        if ahead:
            more = lax.ppermute(made[2], "prop", [(i + 1, i) for i in range(count - 1)])
        velocity, stress, edge = call(
            second_kernel,
            [(3, *shape), (6, *shape), edge_shape],
            (w, far, near, stress, left, shear, masks),
            scratch=[(3, PLANES + 4, EXT, LANES)],
        )
    rec = swap_rows(edge)
    half = (ADV, ROWS, LANES)
    left, grown = call(
        last_plastic_kernel, [(6, *half), (12, *half)], (stress, density, shear, table), flops=HEAVY
    )
    w, message = call(
        last_first_kernel, [wide, (LAST_TILES, 8, LANES)], (velocity, stress, rec, masks, left)
    )
    message = lax.ppermute(message, "prop", [(i + 1, i) for i in range(count - 1)])
    return tuple(
        call(
            last_second_kernel,
            [(3, *shape), (6, *shape), (12, *shape)],
            (w, message, more, stress, rec, left, grown, shear, table, masks, inflow),
            scratch=[(3, PLANES + 4, EXT, LANES)],
        )
    )


def solution(mesh):
    return jax.shard_map(
        local,
        mesh=mesh,
        in_specs=(
            P(None, "prop", "trans", None),
            P(None, "prop", "trans", None),
            P(None, "prop", "trans", None),
            P("prop", "trans", None),
            P(),
            P(),
            P(None, None, "trans", None),
        ),
        out_specs=(
            P(None, "prop", "trans", None),
            P(None, "prop", "trans", None),
            P(None, "prop", "trans", None),
        ),
        check_vma=False,
    )
```

```python
import functools

import jax
import jax.numpy as jnp
from jax import lax
from jax.experimental import pallas as pl
from jax.experimental.pallas import tpu as pltpu
from jax.sharding import PartitionSpec as P

STEPS = 4
ADV = 4
TIME_STEP = 0.15
DRAG_RATE = 0.5
HARDENING = 2.0
RECOVERY = 1.0
VOIGT_PAIRS = ((0, 0), (1, 1), (2, 2), (1, 2), (0, 2), (0, 1))
ACCEL = ((0, 5, 4), (5, 1, 3), (4, 3, 2))

PLANES = 8
ROWS = 16
TAIL = 8
EXT = ROWS + TAIL
LANES = 128
C1 = TIME_STEP / 12.0
C8 = 8.0 * TIME_STEP / 12.0
F32 = jnp.float32


def lane_shifts(x):
    lane = lax.broadcasted_iota(jnp.int32, x.shape, 1)

    def at(offset):
        moved = pltpu.roll(x, (-offset) % LANES, 1)
        inside = lane < LANES - offset if offset > 0 else lane >= -offset
        return jnp.where(inside, moved, 0.0)

    return at(1) - at(-1), at(2) - at(-2)


def row_shifts(x):
    size = x.shape[0]
    return (
        pltpu.roll(x, size - 1, 0) - pltpu.roll(x, 1, 0),
        pltpu.roll(x, size - 2, 0) - pltpu.roll(x, 2, 0),
    )


def extended(inner, tail):
    return jnp.concatenate([inner, tail], axis=0)


def edge_tile(plane):
    row = lax.broadcasted_iota(jnp.int32, (TAIL, LANES), 0)
    return jnp.where(row < 4, plane[:TAIL], plane[ROWS - TAIL :])


def pack_tails(tails, per, mask_ref):
    row = lax.broadcasted_iota(jnp.int32, (TAIL, LANES), 0)
    if per == 4:
        pair = row // 2
        place = jnp.where(mask_ref[4] > 0.5, pair, (pair + 1) % 4)
    else:
        place = jnp.where((row < 2) | (row >= 6), 0, 1)
    tiles = []
    for first in range(0, len(tails), per):
        tile = tails[first]
        for j, tail in enumerate(tails[first : first + per]):
            if j:
                tile = jnp.where(place == j, pltpu.roll(tail, TAIL // per * j, 0), tile)
        tiles.append(tile)
    return tiles


def unpack_tail(tile_at, index, per):
    tile, j = tile_at(index // per), index % per
    return pltpu.roll(tile, TAIL - TAIL // per * j, 0) if j else tile


def plastic_parts(stress, densities, shear, tab_ref):
    doubled = [s if k < 3 else s + s for k, s in enumerate(stress)]
    total = [None] * 6
    grown = []
    for s in range(12):
        coef = [tab_ref[s, k] for k in range(6)]
        coef = [jnp.concatenate([c] * (stress[0].shape[0] // 8), axis=0) for c in coef]
        resolved = doubled[0] * coef[0]
        for k in range(1, 6):
            resolved = resolved + doubled[k] * coef[k]
        density = densities(s)
        rate = (DRAG_RATE * density) * jnp.tanh(resolved)
        for k in range(6):
            term = rate * coef[k]
            total[k] = term if total[k] is None else total[k] + term
        growth = (TIME_STEP * jnp.abs(rate)) * (HARDENING * lax.rsqrt(density) - RECOVERY)
        grown.append(density * jnp.exp(growth))
    scaled = TIME_STEP * shear
    dilation = scaled * (total[0] + total[1] + total[2])
    twice = 2.0 * scaled
    left = [stress[k] - twice * total[k] - (dilation if k < 3 else 0.0) for k in range(6)]
    return left, grown


def stress_change(near, velocity, shear):
    grad = [[None] * 3 for _ in range(3)]
    for c in range(3):
        first = near(c, 1) - near(c, -1)
        second = near(c, 2) - near(c, -2)
        grad[0][c] = 8.0 * first - second
        first, second = row_shifts(velocity[c])
        grad[1][c] = 8.0 * first[:ROWS] - second[:ROWS]
        first, second = lane_shifts(velocity[c][:ROWS])
        grad[2][c] = 8.0 * first - second
    scaled = C1 * shear
    trace = grad[0][0] + grad[1][1] + grad[2][2]
    return [
        scaled * (trace + 2.0 * grad[0][0]),
        scaled * (trace + 2.0 * grad[1][1]),
        scaled * (trace + 2.0 * grad[2][2]),
        scaled * (grad[1][2] + grad[2][1]),
        scaled * (grad[0][2] + grad[2][0]),
        scaled * (grad[0][1] + grad[1][0]),
    ]


def edges_kernel(v_in, s_in, edge_ref, v_ref, s_ref, sems):
    copies = [pltpu.make_async_copy(v_in.at[c], v_ref.at[c], sems.at[c]) for c in range(3)]
    copies += [pltpu.make_async_copy(s_in.at[k], s_ref.at[k], sems.at[3 + k]) for k in range(6)]
    for copy in copies:
        copy.start()
    for k, copy in enumerate(copies):
        copy.wait()
        for p in range(PLANES):
            edge_ref[k, p] = edge_tile(v_ref[k, p] if k < 3 else s_ref[k - 3, p])


def partial_update(p, v_ref, s_ref, rec_ref, below):
    out = []
    for c, (ix, iy, iz) in enumerate(ACCEL):

        def plane(k, q):
            return extended(s_ref[k, q], rec_ref[3 + k, q])

        along = extended(s_ref[iy, p], rec_ref[3 + iy, p] * below)
        first, second = row_shifts(along)
        f, s = lane_shifts(plane(iz, p))
        first, second = first + f, second + s
        if p + 1 < PLANES:
            first = first + plane(ix, p + 1)
        if p - 1 >= 0:
            first = first - plane(ix, p - 1)
        if p + 2 < PLANES:
            second = second + plane(ix, p + 2)
        if p - 2 >= 0:
            second = second - plane(ix, p - 2)
        start = extended(v_ref[c, p], rec_ref[c, p])
        out.append(start + C8 * first - C1 * second)
    return out


def first_kernel(per, v_ref, s_ref, rec_ref, mask_ref, w_ref, near_ref, far_ref):
    below = mask_ref[0]
    even = mask_ref[3] > 0.5
    for p in range(PLANES):
        made = partial_update(p, v_ref, s_ref, rec_ref, below)
        for c in range(3):
            w_ref[c, p] = made[c]
    def both(tile, left, right):
        near_ref[tile] = jnp.where(even, right, left)
        far_ref[tile] = jnp.where(even, left, right)

    low, high = (0, 1), (PLANES - 2, PLANES - 1)
    for c in range(3):
        k = ACCEL[c][0]
        for q in range(2):
            for h in range(2):
                rows = pl.ds(8 * h, 8)
                both(6 * q + 2 * c + h, w_ref[c, low[q], rows], w_ref[c, high[q], rows])
                both(12 + 6 * q + 2 * c + h, s_ref[k, low[q], rows], s_ref[k, high[q], rows])
    packed = [
        pack_tails([rec_ref[3 + ACCEL[c][0], p] for c in range(3) for p in side], per, mask_ref)
        for side in (low, high)
    ]
    for tile, (left, right) in enumerate(zip(*packed)):
        both(24 + tile, left, right)


def plastic_kernel(ahead, s_ref, d_ref, shear_ref, tab_ref, left_ref, grown_ref, *send_ref):
    for p in range(PLANES):
        left, grown = plastic_parts(
            [s_ref[k, p] for k in range(6)], lambda s: d_ref[s, p], shear_ref[p], tab_ref
        )
        for k in range(6):
            left_ref[k, p] = left[k]
        for s in range(12):
            grown_ref[s, p] = grown[s]
            if ahead and p < ADV:
                send_ref[0][s, p] = grown[s]
        if ahead and p < ADV:
            send_ref[0][12, p] = shear_ref[p]


def second_kernel(
    per, w_ref, far_ref, near_ref, s_ref, left_ref, shear_ref, mask_ref, v_ref, out_ref, edge_ref, vel
):
    below, sides = mask_ref[0], (mask_ref[1], mask_ref[2])
    even = mask_ref[3] > 0.5

    def got(side, tile):
        a, b = near_ref[tile], far_ref[tile]
        return jnp.where(even, b, a) if side == 0 else jnp.where(even, a, b)

    def got_w(side, q, c):
        return jnp.concatenate([got(side, 6 * q + 2 * c + h) for h in range(2)], axis=0)

    def got_s(side, q, c):
        tiles = [got(side, 12 + 6 * q + 2 * c + h) for h in range(2)]
        tiles.append(unpack_tail(lambda tile: got(side, 24 + tile), 2 * c + q, per))
        return jnp.concatenate([tile * sides[side] for tile in tiles], axis=0)

    exists = [jnp.concatenate([m, m], axis=0) for m in sides]
    for c in range(3):
        ix = ACCEL[c][0]
        m2, m1, p8, p9 = got_s(0, 0, c), got_s(0, 1, c), got_s(1, 0, c), got_s(1, 1, c)
        for p in range(PLANES):
            value = w_ref[c, p]
            if p == 0:
                value = value - C8 * m1 + C1 * m2
            if p == 1:
                value = value + C1 * m1
            if p == 6:
                value = value - C1 * p8
            if p == 7:
                value = value + C8 * p8 - C1 * p9
            value = extended(value[:ROWS], value[ROWS:] * below)
            vel[c, p + 2] = value
            v_ref[c, p] = value[:ROWS]
            edge_ref[c, p] = edge_tile(value[:ROWS])
        none = jnp.zeros((TAIL, LANES), F32)
        halo = (
            (0, got_w(0, 0, c) - C1 * s_ref[ix, 0], 0),
            (1, got_w(0, 1, c) + C8 * s_ref[ix, 0] - C1 * s_ref[ix, 1], 0),
            (10, got_w(1, 0, c) - C8 * s_ref[ix, 7] + C1 * s_ref[ix, 6], 1),
            (11, got_w(1, 1, c) + C1 * s_ref[ix, 7], 1),
        )
        for at, value, side in halo:
            vel[c, at] = extended(value * exists[side], none)
    for p in range(PLANES):
        change = stress_change(
            lambda c, o: vel[c, p + 2 + o, pl.ds(0, ROWS)], [vel[c, p + 2] for c in range(3)], shear_ref[p]
        )
        for k in range(6):
            value = left_ref[k, p] + change[k]
            out_ref[k, p] = value
            edge_ref[3 + k, p] = edge_tile(value)


LAST_W, LAST_S, LAST_T, LAST_TAILS = 0, 36, 84, 18


def last_first_kernel(per, v_ref, s_ref, rec_ref, mask_ref, unused_ref, w_ref, msg_ref):
    below = mask_ref[0]
    for p in range(PLANES):
        made = partial_update(p, v_ref, s_ref, rec_ref, below)
        for c in range(3):
            w_ref[c, p] = made[c]
            if p < 6:
                for h in range(2):
                    msg_ref[LAST_W + 12 * c + 2 * p + h] = made[c][8 * h : 8 * h + 8]
        if p < ADV:
            for k in range(6):
                for h in range(2):
                    msg_ref[LAST_S + 8 * k + 2 * p + h] = s_ref[k, p, pl.ds(8 * h, 8)]
    tails = [w_ref[c, p, pl.ds(ROWS, TAIL)] for c in range(3) for p in range(ADV)]
    tails += [rec_ref[3 + ACCEL[c][0], p] for c in range(3) for p in range(2)]
    for tile, packed in enumerate(pack_tails(tails, per, mask_ref)):
        msg_ref[LAST_T + tile] = packed


def last_plastic_kernel(s_ref, d_ref, shear_ref, tab_ref, left_ref, grown_ref):
    for p in range(ADV, PLANES):
        left, grown = plastic_parts(
            [s_ref[k, p] for k in range(6)], lambda s: d_ref[s, p], shear_ref[p], tab_ref
        )
        for k in range(6):
            left_ref[k, p - ADV] = left[k]
        for s in range(12):
            grown_ref[s, p - ADV] = grown[s]


def last_second_kernel(
    per, w_ref, msg_ref, more_ref, s_ref, rec_ref, left_ref, grown_ref, shear_ref, tab_ref, mask_ref, inflow_ref,
    v_out, s_out, d_out, vel, v_ref, out_ref, d_ref, sems,
):
    copies = []

    def write(source, target):
        copies.append(pltpu.make_async_copy(source, target, sems.at[len(copies)]))
        copies[-1].start()

    write(grown_ref, d_out.at[:, pl.ds(0, ADV)])
    below = mask_ref[0]
    here = jnp.concatenate([mask_ref[2]] * 2, axis=0)
    inside = here > 0.5

    def got(base, count):
        return jnp.concatenate([msg_ref[base + h] for h in range(count)], axis=0)

    def got_tail(index):
        return unpack_tail(lambda tile: msg_ref[LAST_T + tile], index, per)

    def got_stress(k, p):
        return got(LAST_S + 8 * k + 2 * p, 2)

    for c in range(3):
        ix = ACCEL[c][0]
        p8 = extended(got_stress(ix, 0), got_tail(12 + 2 * c))
        p9 = extended(got_stress(ix, 1), got_tail(12 + 2 * c + 1))
        p6 = extended(s_ref[ix, 6], rec_ref[3 + ix, 6])
        p7 = extended(s_ref[ix, 7], rec_ref[3 + ix, 7])
        for p in range(2, 14):
            if p < PLANES:
                value = w_ref[c, p]
                if p == 6:
                    value = value - C1 * p8
                if p == 7:
                    value = value + C8 * p8 - C1 * p9
            elif p < 12:
                r = p - PLANES
                value = extended(got(LAST_W + 12 * c + 2 * r, 2), got_tail(4 * c + r))
                if p == 8:
                    value = value - C8 * p7 + C1 * p6
                if p == 9:
                    value = value + C1 * p7
            else:
                value = got(LAST_W + 12 * c + 2 * (p - PLANES), 2)
            inner = value[:ROWS]
            tail = value[ROWS:] * below if p < 12 else jnp.zeros((TAIL, LANES), F32)
            if p >= PLANES:
                inner, tail = inner * here, tail * mask_ref[2]
            vel[c, p - 2] = extended(inner, tail)
            if ADV <= p < 12:
                if p >= PLANES:
                    inner = jnp.where(inside, inner, inflow_ref[c, p - PLANES])
                v_ref[c, p - ADV] = inner
    write(v_ref, v_out)
    for q in range(PLANES):
        p = q + ADV
        if p < PLANES:
            left = [left_ref[k, q] for k in range(6)]
            shear = shear_ref[p]
        else:
            r = p - PLANES
            shear = more_ref[12, r]
            left, grown = plastic_parts(
                [got_stress(k, r) for k in range(6)], lambda s: more_ref[s, r], shear, tab_ref
            )
        change = stress_change(
            lambda c, o: vel[c, p - 2 + o, pl.ds(0, ROWS)], [vel[c, p - 2] for c in range(3)], shear
        )
        for k in range(6):
            value = left[k] + change[k]
            if p >= PLANES:
                value = jnp.where(inside, value, inflow_ref[3 + k, p - PLANES])
            out_ref[k, q] = value
        write(out_ref.at[:, q], s_out.at[:, q])
        if p >= PLANES:
            for s in range(12):
                d_ref[s, p - PLANES] = jnp.where(inside, grown[s], inflow_ref[9 + s, p - PLANES])
            write(d_ref.at[:, p - PLANES], d_out.at[:, q])
    for copy in copies:
        copy.wait()


VMEM_LIMIT = 16 * 2**20
HEAVY = 2**34


def call(kernel, outs, args, scratch=(), flops=0):
    return pl.pallas_call(
        kernel,
        out_shape=[jax.ShapeDtypeStruct(shape, F32) for shape in outs],
        scratch_shapes=[pltpu.VMEM(shape, F32) for shape in scratch],
        compiler_params=pltpu.CompilerParams(vmem_limit_bytes=VMEM_LIMIT),
        cost_estimate=pl.CostEstimate(flops=flops, bytes_accessed=2**20, transcendentals=0),
    )(*args)


def schmid_table(normals, directions):
    normal_f = normals.astype(F32)
    direct_f = directions.astype(F32)
    scale = 1.0 / (
        jnp.sqrt(jnp.sum(normal_f * normal_f, 1)) * jnp.sqrt(jnp.sum(direct_f * direct_f, 1))
    )
    columns = [
        0.5 * (direct_f[:, i] * normal_f[:, j] + direct_f[:, j] * normal_f[:, i]) * scale
        for i, j in VOIGT_PAIRS
    ]
    return jnp.stack(columns, 1)


def swap_rows(edge):
    count = lax.axis_size("trans")
    if count == 2:
        return lax.ppermute(edge, "trans", [(0, 1), (1, 0)])
    upper = lax.ppermute(edge[:, :, :4], "trans", [(i + 1, i) for i in range(count - 1)])
    lower = lax.ppermute(edge[:, :, 4:], "trans", [(i, i + 1) for i in range(count - 1)])
    return jnp.concatenate([upper, lower], axis=2)


def all_trade(pairs, count, width):
    partner = {a: b for a, b in pairs} | {b: a for a, b in pairs}
    out = []
    for i in range(count):
        for t in range(width):
            if i in partner:
                out.append((i * width + t, partner[i] * width + t))
            elif t ^ 1 < width:
                out.append((i * width + t, i * width + (t ^ 1)))
    return out


def local(velocity, stress, density, shear, normals, directions, inflow):
    count = lax.axis_size("prop")
    at, side = lax.axis_index("prop"), lax.axis_index("trans")
    table = jnp.broadcast_to(schmid_table(normals, directions)[:, :, None, None], (12, 6, 8, LANES))
    row = lax.broadcasted_iota(jnp.int32, (TAIL, LANES), 0)
    full = jnp.ones((TAIL, LANES), F32)
    masks = jnp.stack(
        [
            jnp.where(row < 4, side < lax.axis_size("trans") - 1, side > 0).astype(F32),
            full * (at > 0).astype(F32),
            full * (at < count - 1).astype(F32),
            full * (at % 2 == 0).astype(F32),
            full * (side < lax.axis_size("trans") - 1).astype(F32),
        ]
    )
    pairs = [(i, i + 1) for i in range(0, count - 1, 2)]
    others = [(i, i + 1) for i in range(1, count - 1, 2)]
    near_swap, far_swap = (all_trade(p, count, lax.axis_size("trans")) for p in (pairs, others))

    per = 4 if lax.axis_size("trans") == 2 else 2
    shape = (PLANES, ROWS, LANES)
    wide = (3, PLANES, EXT, LANES)
    edge_shape = (9, PLANES, TAIL, LANES)
    edge, velocity, stress = pl.pallas_call(
        edges_kernel,
        out_shape=[pltpu.VMEM(d, F32) for d in (edge_shape, (3, *shape), (6, *shape))],
        in_specs=[pl.BlockSpec(memory_space=pltpu.HBM)] * 2,
        scratch_shapes=[pltpu.SemaphoreType.DMA((9,))],
        compiler_params=pltpu.CompilerParams(vmem_limit_bytes=60 * 2**20),
    )(velocity, stress)
    for step in range(STEPS - 1):
        rec = swap_rows(edge)
        message = (24 + -(-6 // per), 8, LANES)
        w, near, far = call(functools.partial(first_kernel, per), [wide, message, message], (velocity, stress, rec, masks))
        far = lax.ppermute(far, ("prop", "trans"), far_swap)
        near = lax.ppermute(near, ("prop", "trans"), near_swap)
        ahead = step == STEPS - 2
        made = call(
            functools.partial(plastic_kernel, ahead),
            [(6, *shape), (12, *shape)] + ([(13, ADV, ROWS, LANES)] if ahead else []),
            (stress, density, shear, table),
            flops=HEAVY,
        )
        left, density = made[:2]
        if ahead:
            more = lax.ppermute(made[2], "prop", [(i + 1, i) for i in range(count - 1)])
        velocity, stress, edge = call(
            functools.partial(second_kernel, per),
            [(3, *shape), (6, *shape), edge_shape],
            (w, far, near, stress, left, shear, masks),
            scratch=[(3, PLANES + 4, EXT, LANES)],
        )
    rec = swap_rows(edge)
    half = (ADV, ROWS, LANES)
    left, grown = call(
        last_plastic_kernel, [(6, *half), (12, *half)], (stress, density, shear, table), flops=HEAVY
    )
    w, message = call(
        functools.partial(last_first_kernel, per),
        [wide, (LAST_T + -(-LAST_TAILS // per), 8, LANES)],
        (velocity, stress, rec, masks, left)
    )
    message = lax.ppermute(message, "prop", [(i + 1, i) for i in range(count - 1)])
    shapes = [(3, *shape), (6, *shape), (12, *shape)]
    return tuple(
        pl.pallas_call(
            functools.partial(last_second_kernel, per),
            out_shape=[jax.ShapeDtypeStruct(d, F32) for d in shapes],
            out_specs=[pl.BlockSpec(memory_space=pl.ANY)] * 3,
            scratch_shapes=[
                pltpu.VMEM((3, PLANES + 4, EXT, LANES), F32),
                *(pltpu.VMEM(d, F32) for d in (*shapes[:2], (12, *half))),
                pltpu.SemaphoreType.DMA((2 + PLANES + ADV,)),
            ],
            compiler_params=pltpu.CompilerParams(vmem_limit_bytes=VMEM_LIMIT),
        )(w, message, more, stress, rec, left, grown, shear, table, masks, inflow)
    )


def solution(mesh):
    return jax.shard_map(
        local,
        mesh=mesh,
        in_specs=(
            P(None, "prop", "trans", None),
            P(None, "prop", "trans", None),
            P(None, "prop", "trans", None),
            P("prop", "trans", None),
            P(),
            P(),
            P(None, None, "trans", None),
        ),
        out_specs=(
            P(None, "prop", "trans", None),
            P(None, "prop", "trans", None),
            P(None, "prop", "trans", None),
        ),
        check_vma=False,
    )
```

```python
import functools

import jax
import jax.numpy as jnp
from jax import lax
from jax.experimental import pallas as pl
from jax.experimental.pallas import tpu as pltpu
from jax.sharding import PartitionSpec as P

STEPS = 4
ADV = 4
TIME_STEP = 0.15
DRAG_RATE = 0.5
HARDENING = 2.0
RECOVERY = 1.0
VOIGT_PAIRS = ((0, 0), (1, 1), (2, 2), (1, 2), (0, 2), (0, 1))
ACCEL = ((0, 5, 4), (5, 1, 3), (4, 3, 2))

PLANES = 8
ROWS = 16
TAIL = 8
EXT = ROWS + TAIL
LANES = 128
C1 = TIME_STEP / 12.0
C8 = 8.0 * TIME_STEP / 12.0
F32 = jnp.float32


def lane_shifts(x):
    lane = lax.broadcasted_iota(jnp.int32, x.shape, 1)

    def at(offset):
        moved = pltpu.roll(x, (-offset) % LANES, 1)
        inside = lane < LANES - offset if offset > 0 else lane >= -offset
        return jnp.where(inside, moved, 0.0)

    return at(1) - at(-1), at(2) - at(-2)


def row_shifts(x):
    size = x.shape[0]
    return (
        pltpu.roll(x, size - 1, 0) - pltpu.roll(x, 1, 0),
        pltpu.roll(x, size - 2, 0) - pltpu.roll(x, 2, 0),
    )


def extended(inner, tail):
    return jnp.concatenate([inner, tail], axis=0)


def edge_tile(plane):
    row = lax.broadcasted_iota(jnp.int32, (TAIL, LANES), 0)
    return jnp.where(row < 4, plane[:TAIL], plane[ROWS - TAIL :])


def pack_tails(tails, per, mask_ref):
    row = lax.broadcasted_iota(jnp.int32, (TAIL, LANES), 0)
    if per == 4:
        pair = row // 2
        place = jnp.where(mask_ref[4] > 0.5, pair, (pair + 1) % 4)
    else:
        place = jnp.where((row < 2) | (row >= 6), 0, 1)
    tiles = []
    for first in range(0, len(tails), per):
        tile = tails[first]
        for j, tail in enumerate(tails[first : first + per]):
            if j:
                tile = jnp.where(place == j, pltpu.roll(tail, TAIL // per * j, 0), tile)
        tiles.append(tile)
    return tiles


def unpack_tail(tile_at, index, per):
    tile, j = tile_at(index // per), index % per
    return pltpu.roll(tile, TAIL - TAIL // per * j, 0) if j else tile


def plastic_parts(stress, densities, shear, tab_ref):
    doubled = [s if k < 3 else s + s for k, s in enumerate(stress)]
    total = [None] * 6
    grown = []
    for s in range(12):
        coef = [tab_ref[s, k] for k in range(6)]
        coef = [jnp.concatenate([c] * (stress[0].shape[0] // 8), axis=0) for c in coef]
        resolved = doubled[0] * coef[0]
        for k in range(1, 6):
            resolved = resolved + doubled[k] * coef[k]
        density = densities(s)
        rate = (DRAG_RATE * density) * jnp.tanh(resolved)
        for k in range(6):
            term = rate * coef[k]
            total[k] = term if total[k] is None else total[k] + term
        growth = (TIME_STEP * jnp.abs(rate)) * (HARDENING * lax.rsqrt(density) - RECOVERY)
        grown.append(density * jnp.exp(growth))
    scaled = TIME_STEP * shear
    dilation = scaled * (total[0] + total[1] + total[2])
    twice = 2.0 * scaled
    left = [stress[k] - twice * total[k] - (dilation if k < 3 else 0.0) for k in range(6)]
    return left, grown


def stress_change(near, velocity, shear):
    grad = [[None] * 3 for _ in range(3)]
    for c in range(3):
        first = near(c, 1) - near(c, -1)
        second = near(c, 2) - near(c, -2)
        grad[0][c] = 8.0 * first - second
        first, second = row_shifts(velocity[c])
        grad[1][c] = 8.0 * first[:ROWS] - second[:ROWS]
        first, second = lane_shifts(velocity[c][:ROWS])
        grad[2][c] = 8.0 * first - second
    scaled = C1 * shear
    trace = grad[0][0] + grad[1][1] + grad[2][2]
    return [
        scaled * (trace + 2.0 * grad[0][0]),
        scaled * (trace + 2.0 * grad[1][1]),
        scaled * (trace + 2.0 * grad[2][2]),
        scaled * (grad[1][2] + grad[2][1]),
        scaled * (grad[0][2] + grad[2][0]),
        scaled * (grad[0][1] + grad[1][0]),
    ]


def edges_kernel(v_in, s_in, edge_ref, v_ref, s_ref, sems):
    copies = [pltpu.make_async_copy(v_in.at[c], v_ref.at[c], sems.at[c]) for c in range(3)]
    copies += [pltpu.make_async_copy(s_in.at[k], s_ref.at[k], sems.at[3 + k]) for k in range(6)]
    for copy in copies:
        copy.start()
    for k, copy in enumerate(copies):
        copy.wait()
        for p in range(PLANES):
            edge_ref[k, p] = edge_tile(v_ref[k, p] if k < 3 else s_ref[k - 3, p])


def partial_update(p, v_ref, s_ref, rec_ref, below):
    out = []
    for c, (ix, iy, iz) in enumerate(ACCEL):

        def plane(k, q):
            return extended(s_ref[k, q], rec_ref[3 + k, q])

        along = extended(s_ref[iy, p], rec_ref[3 + iy, p] * below)
        first, second = row_shifts(along)
        f, s = lane_shifts(plane(iz, p))
        first, second = first + f, second + s
        if p + 1 < PLANES:
            first = first + plane(ix, p + 1)
        if p - 1 >= 0:
            first = first - plane(ix, p - 1)
        if p + 2 < PLANES:
            second = second + plane(ix, p + 2)
        if p - 2 >= 0:
            second = second - plane(ix, p - 2)
        start = extended(v_ref[c, p], rec_ref[c, p])
        out.append(start + C8 * first - C1 * second)
    return out


def first_kernel(per, v_ref, s_ref, rec_ref, mask_ref, *refs):
    w_ref, near_ref, far_ref = refs[-3:]
    below = mask_ref[0]
    even = mask_ref[3] > 0.5
    for p in range(PLANES):
        made = partial_update(p, v_ref, s_ref, rec_ref, below)
        for c in range(3):
            w_ref[c, p] = made[c]
    def both(tile, left, right):
        near_ref[tile] = jnp.where(even, right, left)
        far_ref[tile] = jnp.where(even, left, right)

    low, high = (0, 1), (PLANES - 2, PLANES - 1)
    for c in range(3):
        k = ACCEL[c][0]
        for q in range(2):
            for h in range(2):
                rows = pl.ds(8 * h, 8)
                both(6 * q + 2 * c + h, w_ref[c, low[q], rows], w_ref[c, high[q], rows])
                both(12 + 6 * q + 2 * c + h, s_ref[k, low[q], rows], s_ref[k, high[q], rows])
    packed = [
        pack_tails([rec_ref[3 + ACCEL[c][0], p] for c in range(3) for p in side], per, mask_ref)
        for side in (low, high)
    ]
    for tile, (left, right) in enumerate(zip(*packed)):
        both(24 + tile, left, right)


def plastic_kernel(ahead, s_ref, d_ref, shear_ref, tab_ref, left_ref, grown_ref, *send_ref):
    for p in range(PLANES):
        left, grown = plastic_parts(
            [s_ref[k, p] for k in range(6)], lambda s: d_ref[s, p], shear_ref[p], tab_ref
        )
        for k in range(6):
            left_ref[k, p] = left[k]
        for s in range(12):
            grown_ref[s, p] = grown[s]
            if ahead and p < ADV:
                send_ref[0][s, p] = grown[s]
        if ahead and p < ADV:
            send_ref[0][12, p] = shear_ref[p]


def second_kernel(
    per, w_ref, far_ref, near_ref, s_ref, left_ref, shear_ref, mask_ref, v_ref, out_ref, edge_ref, *refs
):
    send_ref, vel = refs[:-1], refs[-1]
    below, sides = mask_ref[0], (mask_ref[1], mask_ref[2])
    even = mask_ref[3] > 0.5

    def got(side, tile):
        a, b = near_ref[tile], far_ref[tile]
        return jnp.where(even, b, a) if side == 0 else jnp.where(even, a, b)

    def got_w(side, q, c):
        return jnp.concatenate([got(side, 6 * q + 2 * c + h) for h in range(2)], axis=0)

    def got_s(side, q, c):
        tiles = [got(side, 12 + 6 * q + 2 * c + h) for h in range(2)]
        tiles.append(unpack_tail(lambda tile: got(side, 24 + tile), 2 * c + q, per))
        return jnp.concatenate([tile * sides[side] for tile in tiles], axis=0)

    exists = [jnp.concatenate([m, m], axis=0) for m in sides]
    for c in range(3):
        ix = ACCEL[c][0]
        m2, m1, p8, p9 = got_s(0, 0, c), got_s(0, 1, c), got_s(1, 0, c), got_s(1, 1, c)
        for p in range(PLANES):
            value = w_ref[c, p]
            if p == 0:
                value = value - C8 * m1 + C1 * m2
            if p == 1:
                value = value + C1 * m1
            if p == 6:
                value = value - C1 * p8
            if p == 7:
                value = value + C8 * p8 - C1 * p9
            value = extended(value[:ROWS], value[ROWS:] * below)
            vel[c, p + 2] = value
            v_ref[c, p] = value[:ROWS]
            edge_ref[c, p] = edge_tile(value[:ROWS])
        none = jnp.zeros((TAIL, LANES), F32)
        halo = (
            (0, got_w(0, 0, c) - C1 * s_ref[ix, 0], 0),
            (1, got_w(0, 1, c) + C8 * s_ref[ix, 0] - C1 * s_ref[ix, 1], 0),
            (10, got_w(1, 0, c) - C8 * s_ref[ix, 7] + C1 * s_ref[ix, 6], 1),
            (11, got_w(1, 1, c) + C1 * s_ref[ix, 7], 1),
        )
        for at, value, side in halo:
            vel[c, at] = extended(value * exists[side], none)
    for p in range(PLANES):
        change = stress_change(
            lambda c, o: vel[c, p + 2 + o, pl.ds(0, ROWS)], [vel[c, p + 2] for c in range(3)], shear_ref[p]
        )
        for k in range(6):
            value = left_ref[k, p] + change[k]
            out_ref[k, p] = value
            edge_ref[3 + k, p] = edge_tile(value)
            if send_ref and p < ADV:
                send_ref[0][k, p] = value


LAST_W, LAST_T, LAST_TAILS = 0, 36, 18


def last_first_kernel(per, v_ref, s_ref, rec_ref, mask_ref, unused_ref, w_ref, msg_ref):
    below = mask_ref[0]
    for p in range(PLANES):
        made = partial_update(p, v_ref, s_ref, rec_ref, below)
        for c in range(3):
            w_ref[c, p] = made[c]
            if p < 6:
                for h in range(2):
                    msg_ref[LAST_W + 12 * c + 2 * p + h] = made[c][8 * h : 8 * h + 8]
    tails = [w_ref[c, p, pl.ds(ROWS, TAIL)] for c in range(3) for p in range(ADV)]
    tails += [rec_ref[3 + ACCEL[c][0], p] for c in range(3) for p in range(2)]
    for tile, packed in enumerate(pack_tails(tails, per, mask_ref)):
        msg_ref[LAST_T + tile] = packed


def last_plastic_kernel(s_ref, d_ref, shear_ref, tab_ref, left_ref, grown_ref):
    for p in range(ADV, PLANES):
        left, grown = plastic_parts(
            [s_ref[k, p] for k in range(6)], lambda s: d_ref[s, p], shear_ref[p], tab_ref
        )
        for k in range(6):
            left_ref[k, p - ADV] = left[k]
        for s in range(12):
            grown_ref[s, p - ADV] = grown[s]


def next_plastic_kernel(first_ref, more_ref, tab_ref, mask_ref, inflow_ref, left_ref, grown_ref):
    inside = jnp.concatenate([mask_ref[2]] * 2, axis=0) > 0.5
    for p in range(ADV):
        left, grown = plastic_parts(
            [first_ref[k, p] for k in range(6)], lambda s: more_ref[s, p], more_ref[12, p], tab_ref
        )
        for k in range(6):
            left_ref[k, p] = left[k]
        for s in range(12):
            grown_ref[s, p] = jnp.where(inside, grown[s], inflow_ref[9 + s, p])


def last_second_kernel(
    per, w_ref, msg_ref, first_ref, more_ref, s_ref, rec_ref, left_ref, grown_ref, shear_ref, mask_ref, inflow_ref,
    next_left_ref, next_grown_ref,
    v_out, s_out, d_out, vel, v_ref, out_ref, sems,
):
    copies = []

    def write(source, target):
        copies.append(pltpu.make_async_copy(source, target, sems.at[len(copies)]))
        copies[-1].start()

    write(grown_ref, d_out.at[:, pl.ds(0, ADV)])
    write(next_grown_ref, d_out.at[:, pl.ds(ADV, ADV)])
    below = mask_ref[0]
    here = jnp.concatenate([mask_ref[2]] * 2, axis=0)
    inside = here > 0.5

    def got(base, count):
        return jnp.concatenate([msg_ref[base + h] for h in range(count)], axis=0)

    def got_tail(index):
        return unpack_tail(lambda tile: msg_ref[LAST_T + tile], index, per)

    def got_stress(k, p):
        return first_ref[k, p]

    for c in range(3):
        ix = ACCEL[c][0]
        p8 = extended(got_stress(ix, 0), got_tail(12 + 2 * c))
        p9 = extended(got_stress(ix, 1), got_tail(12 + 2 * c + 1))
        p6 = extended(s_ref[ix, 6], rec_ref[3 + ix, 6])
        p7 = extended(s_ref[ix, 7], rec_ref[3 + ix, 7])
        for p in range(2, 14):
            if p < PLANES:
                value = w_ref[c, p]
                if p == 6:
                    value = value - C1 * p8
                if p == 7:
                    value = value + C8 * p8 - C1 * p9
            elif p < 12:
                r = p - PLANES
                value = extended(got(LAST_W + 12 * c + 2 * r, 2), got_tail(4 * c + r))
                if p == 8:
                    value = value - C8 * p7 + C1 * p6
                if p == 9:
                    value = value + C1 * p7
            else:
                value = got(LAST_W + 12 * c + 2 * (p - PLANES), 2)
            inner = value[:ROWS]
            tail = value[ROWS:] * below if p < 12 else jnp.zeros((TAIL, LANES), F32)
            if p >= PLANES:
                inner, tail = inner * here, tail * mask_ref[2]
            vel[c, p - 2] = extended(inner, tail)
            if ADV <= p < 12:
                if p >= PLANES:
                    inner = jnp.where(inside, inner, inflow_ref[c, p - PLANES])
                v_ref[c, p - ADV] = inner
    write(v_ref, v_out)
    for q in range(PLANES):
        p = q + ADV
        if p < PLANES:
            left = [left_ref[k, q] for k in range(6)]
            shear = shear_ref[p]
        else:
            left = [next_left_ref[k, p - PLANES] for k in range(6)]
            shear = more_ref[12, p - PLANES]
        change = stress_change(
            lambda c, o: vel[c, p - 2 + o, pl.ds(0, ROWS)], [vel[c, p - 2] for c in range(3)], shear
        )
        for k in range(6):
            value = left[k] + change[k]
            if p >= PLANES:
                value = jnp.where(inside, value, inflow_ref[3 + k, p - PLANES])
            out_ref[k, q] = value
        write(out_ref.at[:, q], s_out.at[:, q])
    for copy in copies:
        copy.wait()


VMEM_LIMIT = 16 * 2**20
HEAVY = 2**34


def call(kernel, outs, args, scratch=(), flops=0):
    return pl.pallas_call(
        kernel,
        out_shape=[jax.ShapeDtypeStruct(shape, F32) for shape in outs],
        scratch_shapes=[pltpu.VMEM(shape, F32) for shape in scratch],
        compiler_params=pltpu.CompilerParams(vmem_limit_bytes=VMEM_LIMIT),
        cost_estimate=pl.CostEstimate(flops=flops, bytes_accessed=2**20, transcendentals=0),
    )(*args)


def schmid_table(normals, directions):
    normal_f = normals.astype(F32)
    direct_f = directions.astype(F32)
    scale = 1.0 / (
        jnp.sqrt(jnp.sum(normal_f * normal_f, 1)) * jnp.sqrt(jnp.sum(direct_f * direct_f, 1))
    )
    columns = [
        0.5 * (direct_f[:, i] * normal_f[:, j] + direct_f[:, j] * normal_f[:, i]) * scale
        for i, j in VOIGT_PAIRS
    ]
    return jnp.stack(columns, 1)


def swap_rows(edge):
    count = lax.axis_size("trans")
    if count == 2:
        return lax.ppermute(edge, "trans", [(0, 1), (1, 0)])
    upper = lax.ppermute(edge[:, :, :4], "trans", [(i + 1, i) for i in range(count - 1)])
    lower = lax.ppermute(edge[:, :, 4:], "trans", [(i, i + 1) for i in range(count - 1)])
    return jnp.concatenate([upper, lower], axis=2)


def all_trade(pairs, count, width):
    partner = {a: b for a, b in pairs} | {b: a for a, b in pairs}
    out = []
    for i in range(count):
        for t in range(width):
            if i in partner:
                out.append((i * width + t, partner[i] * width + t))
            elif t ^ 1 < width:
                out.append((i * width + t, i * width + (t ^ 1)))
    return out


def local(velocity, stress, density, shear, normals, directions, inflow):
    count = lax.axis_size("prop")
    at, side = lax.axis_index("prop"), lax.axis_index("trans")
    table = jnp.broadcast_to(schmid_table(normals, directions)[:, :, None, None], (12, 6, 8, LANES))
    row = lax.broadcasted_iota(jnp.int32, (TAIL, LANES), 0)
    full = jnp.ones((TAIL, LANES), F32)
    masks = jnp.stack(
        [
            jnp.where(row < 4, side < lax.axis_size("trans") - 1, side > 0).astype(F32),
            full * (at > 0).astype(F32),
            full * (at < count - 1).astype(F32),
            full * (at % 2 == 0).astype(F32),
            full * (side < lax.axis_size("trans") - 1).astype(F32),
        ]
    )
    pairs = [(i, i + 1) for i in range(0, count - 1, 2)]
    others = [(i, i + 1) for i in range(1, count - 1, 2)]
    near_swap, far_swap = (all_trade(p, count, lax.axis_size("trans")) for p in (pairs, others))

    per = 4 if lax.axis_size("trans") == 2 else 2
    shape = (PLANES, ROWS, LANES)
    wide = (3, PLANES, EXT, LANES)
    edge_shape = (9, PLANES, TAIL, LANES)
    edge, velocity, stress = pl.pallas_call(
        edges_kernel,
        out_shape=[pltpu.VMEM(d, F32) for d in (edge_shape, (3, *shape), (6, *shape))],
        in_specs=[pl.BlockSpec(memory_space=pltpu.HBM)] * 2,
        scratch_shapes=[pltpu.SemaphoreType.DMA((9,))],
        compiler_params=pltpu.CompilerParams(vmem_limit_bytes=60 * 2**20),
    )(velocity, stress)
    for step in range(STEPS - 1):
        rec = swap_rows(edge)
        message = (24 + -(-6 // per), 8, LANES)
        ahead = step == STEPS - 2
        made = call(
            functools.partial(plastic_kernel, ahead),
            [(6, *shape), (12, *shape)] + ([(13, ADV, ROWS, LANES)] if ahead else []),
            (stress, density, shear, table),
            flops=HEAVY,
        )
        left, density = made[:2]
        w, near, far = call(
            functools.partial(first_kernel, per),
            [wide, message, message],
            (velocity, stress, rec, masks) + ((left,) if ahead else ()),
        )
        far = lax.ppermute(far, ("prop", "trans"), far_swap)
        near = lax.ppermute(near, ("prop", "trans"), near_swap)
        if ahead:
            more = lax.ppermute(made[2], "prop", [(i + 1, i) for i in range(count - 1)])
        velocity, stress, edge, *first_message = call(
            functools.partial(second_kernel, per),
            [(3, *shape), (6, *shape), edge_shape] + ([(6, ADV, ROWS, LANES)] if ahead else []),
            (w, far, near, stress, left, shear, masks),
            scratch=[(3, PLANES + 4, EXT, LANES)],
        )
    rec = swap_rows(edge)
    half = (ADV, ROWS, LANES)
    left, grown = call(
        last_plastic_kernel, [(6, *half), (12, *half)], (stress, density, shear, table), flops=HEAVY
    )
    w, message = call(
        functools.partial(last_first_kernel, per),
        [wide, (LAST_T + -(-LAST_TAILS // per), 8, LANES)],
        (velocity, stress, rec, masks, left)
    )
    down = [(i + 1, i) for i in range(count - 1)]
    (first,) = (lax.ppermute(m, "prop", down) for m in first_message)
    message = lax.ppermute(message, "prop", down)
    next_left, next_grown = call(
        next_plastic_kernel, [(6, *half), (12, *half)], (first, more, table, masks, inflow), flops=HEAVY
    )
    shapes = [(3, *shape), (6, *shape), (12, *shape)]
    return tuple(
        pl.pallas_call(
            functools.partial(last_second_kernel, per),
            out_shape=[jax.ShapeDtypeStruct(d, F32) for d in shapes],
            out_specs=[pl.BlockSpec(memory_space=pl.ANY)] * 3,
            scratch_shapes=[
                pltpu.VMEM((3, PLANES + 4, EXT, LANES), F32),
                *(pltpu.VMEM(d, F32) for d in shapes[:2]),
                pltpu.SemaphoreType.DMA((3 + PLANES,)),
            ],
            compiler_params=pltpu.CompilerParams(vmem_limit_bytes=VMEM_LIMIT),
        )(w, message, first, more, stress, rec, left, grown, shear, masks, inflow, next_left, next_grown)
    )


def solution(mesh):
    return jax.shard_map(
        local,
        mesh=mesh,
        in_specs=(
            P(None, "prop", "trans", None),
            P(None, "prop", "trans", None),
            P(None, "prop", "trans", None),
            P("prop", "trans", None),
            P(),
            P(),
            P(None, None, "trans", None),
        ),
        out_specs=(
            P(None, "prop", "trans", None),
            P(None, "prop", "trans", None),
            P(None, "prop", "trans", None),
        ),
        check_vma=False,
    )
```

```python
import functools

import jax
import jax.numpy as jnp
from jax import lax
from jax.experimental import pallas as pl
from jax.experimental.pallas import tpu as pltpu
from jax.sharding import PartitionSpec as P

STEPS = 4
ADV = 4
TIME_STEP = 0.15
DRAG_RATE = 0.5
HARDENING = 2.0
RECOVERY = 1.0
VOIGT_PAIRS = ((0, 0), (1, 1), (2, 2), (1, 2), (0, 2), (0, 1))
ACCEL = ((0, 5, 4), (5, 1, 3), (4, 3, 2))

PLANES = 8
ROWS = 16
TAIL = 8
EXT = ROWS + TAIL
LANES = 128
C1 = TIME_STEP / 12.0
C8 = 8.0 * TIME_STEP / 12.0
F32 = jnp.float32


def lane_shifts(x):
    lane = lax.broadcasted_iota(jnp.int32, x.shape, 1)

    def at(offset):
        moved = pltpu.roll(x, (-offset) % LANES, 1)
        inside = lane < LANES - offset if offset > 0 else lane >= -offset
        return jnp.where(inside, moved, 0.0)

    return at(1) - at(-1), at(2) - at(-2)


def row_shifts(x):
    size = x.shape[0]
    return (
        pltpu.roll(x, size - 1, 0) - pltpu.roll(x, 1, 0),
        pltpu.roll(x, size - 2, 0) - pltpu.roll(x, 2, 0),
    )


def extended(inner, tail):
    return jnp.concatenate([inner, tail], axis=0)


def edge_tile(plane):
    row = lax.broadcasted_iota(jnp.int32, (TAIL, LANES), 0)
    return jnp.where(row < 4, plane[:TAIL], plane[ROWS - TAIL :])


def pack_tails(tails, per, mask_ref):
    row = lax.broadcasted_iota(jnp.int32, (TAIL, LANES), 0)
    if per == 4:
        pair = row // 2
        place = jnp.where(mask_ref[4] > 0.5, pair, (pair + 1) % 4)
    else:
        place = jnp.where((row < 2) | (row >= 6), 0, 1)
    tiles = []
    for first in range(0, len(tails), per):
        tile = tails[first]
        for j, tail in enumerate(tails[first : first + per]):
            if j:
                tile = jnp.where(place == j, pltpu.roll(tail, TAIL // per * j, 0), tile)
        tiles.append(tile)
    return tiles


def unpack_tail(tile_at, index, per):
    tile, j = tile_at(index // per), index % per
    return pltpu.roll(tile, TAIL - TAIL // per * j, 0) if j else tile


def plastic_parts(stress, densities, shear, tab_ref):
    doubled = [s if k < 3 else s + s for k, s in enumerate(stress)]
    total = [None] * 6
    grown = []
    for s in range(12):
        coef = [tab_ref[s, k] for k in range(6)]
        coef = [jnp.concatenate([c] * (stress[0].shape[0] // 8), axis=0) for c in coef]
        resolved = doubled[0] * coef[0]
        for k in range(1, 6):
            resolved = resolved + doubled[k] * coef[k]
        density = densities(s)
        rate = (DRAG_RATE * density) * jnp.tanh(resolved)
        for k in range(6):
            term = rate * coef[k]
            total[k] = term if total[k] is None else total[k] + term
        growth = (TIME_STEP * jnp.abs(rate)) * (HARDENING * lax.rsqrt(density) - RECOVERY)
        grown.append(density * jnp.exp(growth))
    scaled = TIME_STEP * shear
    dilation = scaled * (total[0] + total[1] + total[2])
    twice = 2.0 * scaled
    left = [stress[k] - twice * total[k] - (dilation if k < 3 else 0.0) for k in range(6)]
    return left, grown


def stress_change(near, velocity, shear):
    grad = [[None] * 3 for _ in range(3)]
    for c in range(3):
        first = near(c, 1) - near(c, -1)
        second = near(c, 2) - near(c, -2)
        grad[0][c] = 8.0 * first - second
        first, second = row_shifts(velocity[c])
        grad[1][c] = 8.0 * first[:ROWS] - second[:ROWS]
        first, second = lane_shifts(velocity[c][:ROWS])
        grad[2][c] = 8.0 * first - second
    scaled = C1 * shear
    trace = grad[0][0] + grad[1][1] + grad[2][2]
    return [
        scaled * (trace + 2.0 * grad[0][0]),
        scaled * (trace + 2.0 * grad[1][1]),
        scaled * (trace + 2.0 * grad[2][2]),
        scaled * (grad[1][2] + grad[2][1]),
        scaled * (grad[0][2] + grad[2][0]),
        scaled * (grad[0][1] + grad[1][0]),
    ]


def edges_kernel(v_in, s_in, edge_ref, v_ref, s_ref, sems):
    copies = [pltpu.make_async_copy(v_in.at[c], v_ref.at[c], sems.at[c]) for c in range(3)]
    copies += [pltpu.make_async_copy(s_in.at[k], s_ref.at[k], sems.at[3 + k]) for k in range(6)]
    for copy in copies:
        copy.start()
    for k, copy in enumerate(copies):
        copy.wait()
        for p in range(PLANES):
            edge_ref[k, p] = edge_tile(v_ref[k, p] if k < 3 else s_ref[k - 3, p])


def partial_update(p, v_ref, s_ref, rec_ref, below):
    out = []
    for c, (ix, iy, iz) in enumerate(ACCEL):

        def plane(k, q):
            return extended(s_ref[k, q], rec_ref[3 + k, q])

        along = extended(s_ref[iy, p], rec_ref[3 + iy, p] * below)
        first, second = row_shifts(along)
        f, s = lane_shifts(plane(iz, p))
        first, second = first + f, second + s
        if p + 1 < PLANES:
            first = first + plane(ix, p + 1)
        if p - 1 >= 0:
            first = first - plane(ix, p - 1)
        if p + 2 < PLANES:
            second = second + plane(ix, p + 2)
        if p - 2 >= 0:
            second = second - plane(ix, p - 2)
        start = extended(v_ref[c, p], rec_ref[c, p])
        out.append(start + C8 * first - C1 * second)
    return out


def first_kernel(per, v_ref, s_ref, rec_ref, mask_ref, w_ref, near_ref, far_ref):
    below = mask_ref[0]
    even = mask_ref[3] > 0.5
    for p in range(PLANES):
        made = partial_update(p, v_ref, s_ref, rec_ref, below)
        for c in range(3):
            w_ref[c, p] = made[c]
    def both(tile, left, right):
        near_ref[tile] = jnp.where(even, right, left)
        far_ref[tile] = jnp.where(even, left, right)

    low, high = (0, 1), (PLANES - 2, PLANES - 1)
    for c in range(3):
        k = ACCEL[c][0]
        for q in range(2):
            for h in range(2):
                rows = pl.ds(8 * h, 8)
                both(6 * q + 2 * c + h, w_ref[c, low[q], rows], w_ref[c, high[q], rows])
                both(12 + 6 * q + 2 * c + h, s_ref[k, low[q], rows], s_ref[k, high[q], rows])
    packed = [
        pack_tails([rec_ref[3 + ACCEL[c][0], p] for c in range(3) for p in side], per, mask_ref)
        for side in (low, high)
    ]
    for tile, (left, right) in enumerate(zip(*packed)):
        both(24 + tile, left, right)


def plastic_kernel(ahead, s_ref, d_ref, shear_ref, tab_ref, left_ref, grown_ref, *send_ref):
    for p in range(PLANES):
        left, grown = plastic_parts(
            [s_ref[k, p] for k in range(6)], lambda s: d_ref[s, p], shear_ref[p], tab_ref
        )
        for k in range(6):
            left_ref[k, p] = left[k]
        for s in range(12):
            grown_ref[s, p] = grown[s]
            if ahead and p < ADV:
                send_ref[0][s, p] = grown[s]
        if ahead and p < ADV:
            send_ref[0][12, p] = shear_ref[p]


def second_kernel(
    per, w_ref, far_ref, near_ref, s_ref, left_ref, shear_ref, mask_ref, v_ref, out_ref, edge_ref, *refs
):
    send_ref, vel = refs[:-1], refs[-1]
    below, sides = mask_ref[0], (mask_ref[1], mask_ref[2])
    even = mask_ref[3] > 0.5

    def got(side, tile):
        a, b = near_ref[tile], far_ref[tile]
        return jnp.where(even, b, a) if side == 0 else jnp.where(even, a, b)

    def got_w(side, q, c):
        return jnp.concatenate([got(side, 6 * q + 2 * c + h) for h in range(2)], axis=0)

    def got_s(side, q, c):
        tiles = [got(side, 12 + 6 * q + 2 * c + h) for h in range(2)]
        tiles.append(unpack_tail(lambda tile: got(side, 24 + tile), 2 * c + q, per))
        return jnp.concatenate([tile * sides[side] for tile in tiles], axis=0)

    exists = [jnp.concatenate([m, m], axis=0) for m in sides]
    for c in range(3):
        ix = ACCEL[c][0]
        m2, m1, p8, p9 = got_s(0, 0, c), got_s(0, 1, c), got_s(1, 0, c), got_s(1, 1, c)
        for p in range(PLANES):
            value = w_ref[c, p]
            if p == 0:
                value = value - C8 * m1 + C1 * m2
            if p == 1:
                value = value + C1 * m1
            if p == 6:
                value = value - C1 * p8
            if p == 7:
                value = value + C8 * p8 - C1 * p9
            value = extended(value[:ROWS], value[ROWS:] * below)
            vel[c, p + 2] = value
            v_ref[c, p] = value[:ROWS]
            edge_ref[c, p] = edge_tile(value[:ROWS])
        none = jnp.zeros((TAIL, LANES), F32)
        halo = (
            (0, got_w(0, 0, c) - C1 * s_ref[ix, 0], 0),
            (1, got_w(0, 1, c) + C8 * s_ref[ix, 0] - C1 * s_ref[ix, 1], 0),
            (10, got_w(1, 0, c) - C8 * s_ref[ix, 7] + C1 * s_ref[ix, 6], 1),
            (11, got_w(1, 1, c) + C1 * s_ref[ix, 7], 1),
        )
        for at, value, side in halo:
            vel[c, at] = extended(value * exists[side], none)
    for p in range(PLANES):
        change = stress_change(
            lambda c, o: vel[c, p + 2 + o, pl.ds(0, ROWS)], [vel[c, p + 2] for c in range(3)], shear_ref[p]
        )
        for k in range(6):
            value = left_ref[k, p] + change[k]
            out_ref[k, p] = value
            edge_ref[3 + k, p] = edge_tile(value)
            if send_ref and p < ADV:
                send_ref[0][k, p] = value


LAST_W, LAST_T, LAST_TAILS = 0, 36, 18


def last_first_kernel(per, v_ref, s_ref, rec_ref, mask_ref, unused_ref, w_ref, msg_ref):
    below = mask_ref[0]
    for p in range(PLANES):
        made = partial_update(p, v_ref, s_ref, rec_ref, below)
        for c in range(3):
            w_ref[c, p] = made[c]
            if p < 6:
                for h in range(2):
                    msg_ref[LAST_W + 12 * c + 2 * p + h] = made[c][8 * h : 8 * h + 8]
    tails = [w_ref[c, p, pl.ds(ROWS, TAIL)] for c in range(3) for p in range(ADV)]
    tails += [rec_ref[3 + ACCEL[c][0], p] for c in range(3) for p in range(2)]
    for tile, packed in enumerate(pack_tails(tails, per, mask_ref)):
        msg_ref[LAST_T + tile] = packed


def last_plastic_kernel(s_ref, d_ref, shear_ref, tab_ref, left_ref, grown_ref):
    for p in range(ADV, PLANES):
        left, grown = plastic_parts(
            [s_ref[k, p] for k in range(6)], lambda s: d_ref[s, p], shear_ref[p], tab_ref
        )
        for k in range(6):
            left_ref[k, p - ADV] = left[k]
        for s in range(12):
            grown_ref[s, p - ADV] = grown[s]


def next_plastic_kernel(first_ref, more_ref, tab_ref, mask_ref, inflow_ref, left_ref, grown_ref):
    inside = jnp.concatenate([mask_ref[2]] * 2, axis=0) > 0.5
    for p in range(ADV):
        left, grown = plastic_parts(
            [first_ref[k, p] for k in range(6)], lambda s: more_ref[s, p], more_ref[12, p], tab_ref
        )
        for k in range(6):
            left_ref[k, p] = left[k]
        for s in range(12):
            grown_ref[s, p] = jnp.where(inside, grown[s], inflow_ref[9 + s, p])


def last_second_kernel(
    per, w_ref, msg_ref, first_ref, more_ref, s_ref, rec_ref, left_ref, grown_ref, shear_ref, mask_ref, inflow_ref,
    next_left_ref, next_grown_ref,
    v_out, s_out, d_out, vel, v_ref, out_ref, sems,
):
    copies = []

    def write(source, target):
        copies.append(pltpu.make_async_copy(source, target, sems.at[len(copies)]))
        copies[-1].start()

    write(grown_ref, d_out.at[:, pl.ds(0, ADV)])
    write(next_grown_ref, d_out.at[:, pl.ds(ADV, ADV)])
    below = mask_ref[0]
    here = jnp.concatenate([mask_ref[2]] * 2, axis=0)
    inside = here > 0.5

    def got(base, count):
        return jnp.concatenate([msg_ref[base + h] for h in range(count)], axis=0)

    def got_tail(index):
        return unpack_tail(lambda tile: msg_ref[LAST_T + tile], index, per)

    def got_stress(k, p):
        return first_ref[k, p]

    for c in range(3):
        ix = ACCEL[c][0]
        p8 = extended(got_stress(ix, 0), got_tail(12 + 2 * c))
        p9 = extended(got_stress(ix, 1), got_tail(12 + 2 * c + 1))
        p6 = extended(s_ref[ix, 6], rec_ref[3 + ix, 6])
        p7 = extended(s_ref[ix, 7], rec_ref[3 + ix, 7])
        for p in range(2, 14):
            if p < PLANES:
                value = w_ref[c, p]
                if p == 6:
                    value = value - C1 * p8
                if p == 7:
                    value = value + C8 * p8 - C1 * p9
            elif p < 12:
                r = p - PLANES
                value = extended(got(LAST_W + 12 * c + 2 * r, 2), got_tail(4 * c + r))
                if p == 8:
                    value = value - C8 * p7 + C1 * p6
                if p == 9:
                    value = value + C1 * p7
            else:
                value = got(LAST_W + 12 * c + 2 * (p - PLANES), 2)
            inner = value[:ROWS]
            tail = value[ROWS:] * below if p < 12 else jnp.zeros((TAIL, LANES), F32)
            if p >= PLANES:
                inner, tail = inner * here, tail * mask_ref[2]
            vel[c, p - 2] = extended(inner, tail)
            if ADV <= p < 12:
                if p >= PLANES:
                    inner = jnp.where(inside, inner, inflow_ref[c, p - PLANES])
                v_ref[c, p - ADV] = inner
    write(v_ref, v_out)
    for q in range(PLANES):
        p = q + ADV
        if p < PLANES:
            left = [left_ref[k, q] for k in range(6)]
            shear = shear_ref[p]
        else:
            left = [next_left_ref[k, p - PLANES] for k in range(6)]
            shear = more_ref[12, p - PLANES]
        change = stress_change(
            lambda c, o: vel[c, p - 2 + o, pl.ds(0, ROWS)], [vel[c, p - 2] for c in range(3)], shear
        )
        for k in range(6):
            value = left[k] + change[k]
            if p >= PLANES:
                value = jnp.where(inside, value, inflow_ref[3 + k, p - PLANES])
            out_ref[k, q] = value
        write(out_ref.at[:, q], s_out.at[:, q])
    for copy in copies:
        copy.wait()


VMEM_LIMIT = 16 * 2**20
HEAVY = 2**34


def call(kernel, outs, args, scratch=(), flops=0):
    return pl.pallas_call(
        kernel,
        out_shape=[jax.ShapeDtypeStruct(shape, F32) for shape in outs],
        scratch_shapes=[pltpu.VMEM(shape, F32) for shape in scratch],
        compiler_params=pltpu.CompilerParams(vmem_limit_bytes=VMEM_LIMIT),
        cost_estimate=pl.CostEstimate(flops=flops, bytes_accessed=2**20, transcendentals=0),
    )(*args)


def schmid_table(normals, directions):
    normal_f = normals.astype(F32)
    direct_f = directions.astype(F32)
    scale = 1.0 / (
        jnp.sqrt(jnp.sum(normal_f * normal_f, 1)) * jnp.sqrt(jnp.sum(direct_f * direct_f, 1))
    )
    columns = [
        0.5 * (direct_f[:, i] * normal_f[:, j] + direct_f[:, j] * normal_f[:, i]) * scale
        for i, j in VOIGT_PAIRS
    ]
    return jnp.stack(columns, 1)


def swap_rows(edge):
    count = lax.axis_size("trans")
    if count == 2:
        return lax.ppermute(edge, "trans", [(0, 1), (1, 0)])
    upper = lax.ppermute(edge[:, :, :4], "trans", [(i + 1, i) for i in range(count - 1)])
    lower = lax.ppermute(edge[:, :, 4:], "trans", [(i, i + 1) for i in range(count - 1)])
    return jnp.concatenate([upper, lower], axis=2)


def all_trade(pairs, count, width):
    partner = {a: b for a, b in pairs} | {b: a for a, b in pairs}
    out = []
    for i in range(count):
        for t in range(width):
            if i in partner:
                out.append((i * width + t, partner[i] * width + t))
            elif t ^ 1 < width:
                out.append((i * width + t, i * width + (t ^ 1)))
    return out


def local(velocity, stress, density, shear, normals, directions, inflow):
    count = lax.axis_size("prop")
    at, side = lax.axis_index("prop"), lax.axis_index("trans")
    table = jnp.broadcast_to(schmid_table(normals, directions)[:, :, None, None], (12, 6, 8, LANES))
    row = lax.broadcasted_iota(jnp.int32, (TAIL, LANES), 0)
    full = jnp.ones((TAIL, LANES), F32)
    masks = jnp.stack(
        [
            jnp.where(row < 4, side < lax.axis_size("trans") - 1, side > 0).astype(F32),
            full * (at > 0).astype(F32),
            full * (at < count - 1).astype(F32),
            full * (at % 2 == 0).astype(F32),
            full * (side < lax.axis_size("trans") - 1).astype(F32),
        ]
    )
    pairs = [(i, i + 1) for i in range(0, count - 1, 2)]
    others = [(i, i + 1) for i in range(1, count - 1, 2)]
    near_swap, far_swap = (all_trade(p, count, lax.axis_size("trans")) for p in (pairs, others))

    per = 4 if lax.axis_size("trans") == 2 else 2
    shape = (PLANES, ROWS, LANES)
    wide = (3, PLANES, EXT, LANES)
    edge_shape = (9, PLANES, TAIL, LANES)
    edge, velocity, stress = pl.pallas_call(
        edges_kernel,
        out_shape=[pltpu.VMEM(d, F32) for d in (edge_shape, (3, *shape), (6, *shape))],
        in_specs=[pl.BlockSpec(memory_space=pltpu.HBM)] * 2,
        scratch_shapes=[pltpu.SemaphoreType.DMA((9,))],
        compiler_params=pltpu.CompilerParams(vmem_limit_bytes=60 * 2**20),
    )(velocity, stress)
    for step in range(STEPS - 1):
        rec = swap_rows(edge)
        message = (24 + -(-6 // per), 8, LANES)
        w, near, far = call(
            functools.partial(first_kernel, per), [wide, message, message], (velocity, stress, rec, masks)
        )
        far = lax.ppermute(far, ("prop", "trans"), far_swap)
        near = lax.ppermute(near, ("prop", "trans"), near_swap)
        ahead = step == STEPS - 2
        made = call(
            functools.partial(plastic_kernel, ahead),
            [(6, *shape), (12, *shape)] + ([(13, ADV, ROWS, LANES)] if ahead else []),
            (stress, density, shear, table),
            flops=HEAVY,
        )
        left, density = made[:2]
        if ahead:
            more = lax.ppermute(made[2], "prop", [(i + 1, i) for i in range(count - 1)])
        velocity, stress, edge, *first_message = call(
            functools.partial(second_kernel, per),
            [(3, *shape), (6, *shape), edge_shape] + ([(6, ADV, ROWS, LANES)] if ahead else []),
            (w, far, near, stress, left, shear, masks),
            scratch=[(3, PLANES + 4, EXT, LANES)],
        )
    rec = swap_rows(edge)
    half = (ADV, ROWS, LANES)
    left, grown = call(
        last_plastic_kernel, [(6, *half), (12, *half)], (stress, density, shear, table), flops=HEAVY
    )
    w, message = call(
        functools.partial(last_first_kernel, per),
        [wide, (LAST_T + -(-LAST_TAILS // per), 8, LANES)],
        (velocity, stress, rec, masks, left)
    )
    down = [(i + 1, i) for i in range(count - 1)]
    (first,) = (lax.ppermute(m, "prop", down) for m in first_message)
    message = lax.ppermute(message, "prop", down)
    next_left, next_grown = call(
        next_plastic_kernel, [(6, *half), (12, *half)], (first, more, table, masks, inflow), flops=HEAVY
    )
    shapes = [(3, *shape), (6, *shape), (12, *shape)]
    return tuple(
        pl.pallas_call(
            functools.partial(last_second_kernel, per),
            out_shape=[jax.ShapeDtypeStruct(d, F32) for d in shapes],
            out_specs=[pl.BlockSpec(memory_space=pl.ANY)] * 3,
            scratch_shapes=[
                pltpu.VMEM((3, PLANES + 4, EXT, LANES), F32),
                *(pltpu.VMEM(d, F32) for d in shapes[:2]),
                pltpu.SemaphoreType.DMA((3 + PLANES,)),
            ],
            compiler_params=pltpu.CompilerParams(vmem_limit_bytes=VMEM_LIMIT),
        )(w, message, first, more, stress, rec, left, grown, shear, masks, inflow, next_left, next_grown)
    )


def solution(mesh):
    return jax.shard_map(
        local,
        mesh=mesh,
        in_specs=(
            P(None, "prop", "trans", None),
            P(None, "prop", "trans", None),
            P(None, "prop", "trans", None),
            P("prop", "trans", None),
            P(),
            P(),
            P(None, None, "trans", None),
        ),
        out_specs=(
            P(None, "prop", "trans", None),
            P(None, "prop", "trans", None),
            P(None, "prop", "trans", None),
        ),
        check_vma=False,
    )
```
